32 devices in a mesh: seq: 16 (over z, x, core), head: 2 (over y).
Axes of the slice: x: 2, y: 2, z: 4, core: 2. Of those that a mesh axis runs over, the one named last changes fastest.
Arguments:
- queries: bfloat16 [16384, 4096], P('seq', 'head'), may hold values from -0.5 to 0.5
- key_rows: bfloat16 [16384, 4096], P('seq', 'head'), may hold values from -6 to 6
- value_rows: bfloat16 [16384, 4096], P('seq', 'head'), may hold values from -6 to 6
- decay_rates: float32 [32], P('head'), as said below
- out_gain: float32 [4096], P('head'), may hold values from 0.5 to 1.5
Outputs:
- attended: bfloat16 [16384, 4096], P('seq', 'head')
The draws below stay inside these ranges and needn't reach their ends.
Inputs may be any that keep to these rules, and one draw needn't show every extreme that they name: `decay_rates`: positive per-head decay rates.
All inputs are finite; a program needn't handle non-finite values.
Results may differ from the reference program's by a relative error of at most 0.0054.
Values sent between devices are 32-bit elements; how exact they have to be, the bound alone decides.
A program may use at most 128 MiB of HBM per device.

```python
import jax
import jax.numpy as jnp
from jax import lax

H = 32
E = 128
BLOCK = 256
TOKENS = 16384
BLOCKS = 64


def draw_decay_rates(key, part):
    order_key = jax.random.fold_in(key, 11)
    slow_key = jax.random.fold_in(key, 12)
    fast_key = jax.random.fold_in(key, 13)
    head_ranks = jax.random.permutation(order_key, H)
    slow_heads = head_ranks < H // 2
    slow_rate = jnp.exp(jax.random.uniform(slow_key, (H,), jnp.float32, jnp.log(0.25), jnp.log(2.0))) / TOKENS
    fast_rate = jnp.exp(jax.random.uniform(fast_key, (H,), jnp.float32, jnp.log(1.0 / 50.0), jnp.log(1.0 / 30.0)))
    return jnp.where(slow_heads, slow_rate, fast_rate).astype(jnp.float32)


def block_scale(stream_key, extent, cuts, low, top_value):
    def one(dim, shards_of):
        heights = jax.random.uniform(jax.random.fold_in(jax.random.fold_in(stream_key, 6), dim), (shards_of,), jnp.float32, low / len(cuts), top_value / len(cuts))
        return jnp.repeat(jnp.exp(heights), extent[dim] // shards_of).reshape((-1,) + (1,) * (len(extent) - dim - 1))

    gain = one(*cuts[0])
    for cut in cuts[1:]:
        gain = gain * one(*cut)
    return gain


def noise(own_key, shape, spread, most, split=(), held_as=jnp.bfloat16):
    entries = spread * jax.random.normal(own_key, shape, jnp.float32)
    if split:
        entries = entries * block_scale(own_key, shape, split, -0.22, 0.18)
    return jnp.clip(entries, -most, most).astype(held_as)


def setup_inputs(seed: int = 0) -> dict:
    arg_keys = jax.random.split(jax.random.key(seed), 6)
    return {
        "queries": noise(arg_keys[0], (TOKENS, H * E), E ** -0.5, 0.5, ((0, 16), (1, 2))),
        "key_rows": noise(arg_keys[1], (TOKENS, H * E), 1.0, 6.0, ((0, 16), (1, 2))),
        "value_rows": noise(arg_keys[2], (TOKENS, H * E), 1.0, 6.0, ((0, 16), (1, 2))),
        "decay_rates": draw_decay_rates(jax.random.fold_in(arg_keys[5], 71), 0),
        "out_gain": jnp.clip(1.0 + 0.1 * jax.random.normal(arg_keys[4], (H * E,), jnp.float32), 0.5, 1.5),
    }


EPSILON = 1e-06

def to_half(value_matrix):
    return lax.optimization_barrier(value_matrix.astype(jnp.bfloat16)).astype(jnp.float32)

def reference(queries, key_rows, value_rows, decay_rates, out_gain):
    log_decay = -decay_rates.astype(jnp.float32)
    positions = jnp.arange(BLOCK).astype(jnp.float32)
    distance = positions[:, None] - positions[None, :]
    masked = jnp.where(distance[None] >= 0, jnp.exp(log_decay[:, None, None] * jnp.maximum(distance, 0.0)[None]), 0.0)
    key_scale = jnp.exp(log_decay[None, :] * (BLOCK - 1 - positions)[:, None])
    query_scale = jnp.exp(log_decay[None, :] * (positions + 1.0)[:, None])
    block_decay = jnp.exp(log_decay * BLOCK)
    gain_heads = out_gain.reshape(H, E).astype(jnp.float32)
    shaped = (queries.reshape(BLOCKS, BLOCK, H, E), key_rows.reshape(BLOCKS, BLOCK, H, E), value_rows.reshape(BLOCKS, BLOCK, H, E))

    def block_step(carry_state, block):
        query_block = block[0].astype(jnp.float32)
        key_block = block[1].astype(jnp.float32)
        current_value_block = block[2].astype(jnp.float32)
        scores = jnp.einsum('qhe,khe->hqk', query_block, key_block)
        local_out = jnp.einsum('hqk,khe->qhe', to_half(scores * masked), current_value_block)
        carried_out = jnp.einsum('qhe,hef->qhf', query_block, to_half(carry_state)) * query_scale[:, :, None]
        mixed = local_out + carried_out
        decay_scaled_keys = to_half(key_block * key_scale[:, :, None])
        per_block_state = jnp.einsum('tap,tax->apx', decay_scaled_keys, current_value_block)
        next_state = block_decay[:, None, None] * carry_state + per_block_state
        inverse = lax.rsqrt(lax.optimization_barrier(jnp.mean(mixed * mixed, axis=(1, 2))) + EPSILON)
        attended = (mixed * inverse[:, None, None] * gain_heads[None]).astype(jnp.bfloat16)
        return (next_state, attended)
    initial_state = jnp.zeros((H, E, E), jnp.float32)
    _, outputs = lax.scan(block_step, initial_state, shaped)
    return outputs.reshape(TOKENS, H * E)
```

```python
import functools

import jax
import jax.numpy as jnp
from jax import lax
from jax.experimental import pallas as pl
from jax.experimental.pallas import tpu as pltpu
from jax.sharding import PartitionSpec as P

E = 128
BLOCK = 256
EPSILON = 1e-06
GROUP = 4
F32 = jnp.float32
BF16 = jnp.bfloat16


def dot(a, b, contract):
    return lax.dot_general(a, b, ((contract[:1], contract[1:]), ((), ())), preferred_element_type=F32)


def kernel(
    runs, ways, heads_all,
    q_hbm, k_hbm, v_hbm, rates, gain, out_hbm,
    q_buf, k_buf, v_buf, o_buf, mix, acc, entering,
    s_loc, s_oth, c_tot, c_oth, p_in, p_out, e_mine, e_send, e_oth, ss_loc, ss_in,
    q_sem, k_sem, v_sem, o_sem, s_ss, s_rs, c_ss, c_rs, p_ss, p_rs, e_ss, e_rs, n_ss, n_rs,
):
    heads, length = q_buf.shape[0], q_buf.shape[1]
    half = heads // 2
    blocks = length // BLOCK
    groups = runs // GROUP
    me = lax.axis_index("seq")
    way = lax.axis_index("head")
    core = lax.rem(me, 2)
    x = lax.rem(me // 2, 2)
    z = me // GROUP
    core_peer = me + 1 - 2 * core
    x_peer = me + 2 - 4 * x
    own0 = core * half
    oth0 = (1 - core) * half
    core_f = core.astype(F32)
    x_f = x.astype(F32)

    def load(hbm, buf, sem, h):
        return pltpu.make_async_copy(hbm.at[:, pl.ds(pl.multiple_of(h * E, E), E)], buf.at[h], sem.at[h])

    def store(h):
        return pltpu.make_async_copy(o_buf.at[h], out_hbm.at[:, pl.ds(pl.multiple_of(h * E, E), E)], o_sem.at[h])

    def remote(src, dst, ss, rs, seq, head):
        return pltpu.make_async_remote_copy(
            src_ref=src, dst_ref=dst, send_sem=ss, recv_sem=rs,
            device_id={"seq": seq, "head": head}, device_id_type=pl.DeviceIdType.MESH,
        )

    def state_copy(k):
        return remote(s_loc.at[oth0 + k], s_oth.at[k], s_ss.at[k], s_rs.at[k], core_peer, way)

    def chip_copy(k):
        return remote(c_tot.at[k], c_oth.at[k], c_ss.at[k], c_rs.at[k], x_peer, way)

    def chain_copy(k):
        up = lax.rem(me + GROUP, runs)
        return remote(p_out.at[k], p_in.at[k], p_ss.at[k], p_rs.at[k], up, way)

    def carry_copy(k):
        return remote(e_send.at[k], e_oth.at[k], e_ss.at[k], e_rs.at[k], core_peer, way)

    def norm_copy(d):
        return remote(ss_loc, ss_in.at[d - 1], n_ss.at[d - 1], n_rs.at[d - 1], me, lax.rem(way + d, ways))

    def start_states(k, c):
        for h in (own0 + k, oth0 + k):
            load(k_hbm, k_buf, k_sem, h).start()
            load(v_hbm, v_buf, v_sem, h).start()
        return c

    def start_queries(k, c):
        for h in (own0 + k, oth0 + k):
            load(q_hbm, q_buf, q_sem, h).start()
        return c

    lax.fori_loop(0, half, start_states, 0)
    lax.fori_loop(0, half, start_queries, 0)

    barrier = pltpu.get_barrier_semaphore()

    def greet(seq, head):
        pl.semaphore_signal(
            barrier, inc=1, device_id={"seq": seq, "head": head}, device_id_type=pl.DeviceIdType.MESH
        )

    greet(core_peer, way)
    greet(x_peer, way)
    for d in range(1, ways):
        greet(me, lax.rem(way + d, ways))

    @pl.when(z > 0)
    def _():
        greet(me - GROUP, way)

    @pl.when(z < groups - 1)
    def _():
        greet(me + GROUP, way)

    @pl.when(z == 0)
    def _():
        p_in[...] = jnp.zeros_like(p_in)

    acc[...] = jnp.zeros_like(acc)
    pl.semaphore_wait(barrier, 2 + (ways - 1) + jnp.minimum(z, 1) + jnp.minimum(groups - 1 - z, 1))

    def power(rate, steps):
        return jnp.exp(jnp.full((1, E), -rate * steps, F32))

    row = lax.broadcasted_iota(jnp.int32, (BLOCK, E), 0).astype(F32)

    def local_state(h):
        rate = rates[h]
        load(k_hbm, k_buf, k_sem, h).wait()
        load(v_hbm, v_buf, v_sem, h).wait()
        scale = jnp.exp(-rate * (BLOCK - 1 - row))
        whole = power(rate, float(BLOCK))
        state = None
        for b in range(blocks):
            rows = pl.ds(b * BLOCK, BLOCK)
            scaled = (k_buf[h, rows, :].astype(F32) * scale).astype(BF16)
            part = dot(scaled, v_buf[h, rows, :], (0, 0))
            state = part if state is None else state * whole + part
            if b < blocks - 1:
                entering[h, b] = state
        s_loc[h] = state

    def chip_total(k):
        rate = rates[own0 + k]
        state_copy(k).wait_recv()
        mine = power(rate, length * (1.0 - core_f))
        other = power(rate, length * core_f)
        c_tot[k] = mine * s_loc[own0 + k] + other * s_oth[k]
        chip_copy(k).start()

    def state_step(k, c):
        local_state(oth0 + k)
        state_copy(k).start()
        local_state(own0 + k)

        @pl.when(k > 0)
        def _():
            chip_total(k - 1)

        return c

    lax.fori_loop(0, half, state_step, 0)
    chip_total(half - 1)

    small = E
    down = lax.broadcasted_iota(jnp.int32, (small, small), 0) - lax.broadcasted_iota(jnp.int32, (small, small), 1)
    down_f = down.astype(F32)

    def attend(h):
        rate = rates[h]
        load(q_hbm, q_buf, q_sem, h).wait()
        near = jnp.where(down >= 0, jnp.exp(-rate * jnp.maximum(down_f, 0.0)), 0.0)
        far = jnp.exp(-rate * (down_f + small))
        for b in range(blocks):
            rows = pl.ds(b * BLOCK, BLOCK)
            vals = v_buf[h, rows, :]
            scores = dot(q_buf[h, rows, :], k_buf[h, rows, :], (1, 1))
            top = (scores[:small, :small] * near).astype(BF16)
            low = jnp.concatenate(
                [(scores[small:, :small] * far).astype(BF16), (scores[small:, small:] * near).astype(BF16)], axis=1
            )
            mix[h, pl.ds(b * BLOCK, small), :] = dot(top, vals[:small], (1, 0))
            mix[h, pl.ds(b * BLOCK + small, small), :] = dot(low, vals, (1, 0))

    def chain(k):
        rate = rates[own0 + k]
        chip_copy(k).wait_recv()

        @pl.when(z > 0)
        def _():
            chain_copy(k).wait_recv()

        before = p_in[k]
        other = c_oth[k]
        two = 2.0 * length

        @pl.when(z < groups - 1)
        def _():
            total = power(rate, two * (1.0 - x_f)) * c_tot[k] + power(rate, two * x_f) * other
            p_out[k] = power(rate, 2.0 * two) * before + total
            chain_copy(k).start()

        chip = power(rate, two * x_f) * before + x_f * other

        @pl.when(core == 0)
        def _():
            e_mine[k] = chip
            e_send[k] = power(rate, float(length)) * chip + s_loc[own0 + k]

        @pl.when(core == 1)
        def _():
            e_mine[k] = power(rate, float(length)) * chip + s_oth[k]
            e_send[k] = chip

        carry_copy(k).start()

    def finish(h, carry):
        rate = rates[h]
        scale = jnp.exp(-rate * (row + 1.0))
        for b in range(blocks):
            rows = pl.ds(b * BLOCK, BLOCK)
            state = carry
            if b > 0:
                state = power(rate, float(b * BLOCK)) * carry + entering[h, b - 1]
            mixed = mix[h, rows, :] + scale * dot(q_buf[h, rows, :], state.astype(BF16), (1, 0))
            mix[h, rows, :] = mixed
            acc[rows, :] += mixed * mixed

    top_lag = min(3 * (groups - 1), half)
    lag = jnp.minimum(3 * z, half)

    def step(i, c):
        @pl.when(i < half)
        def _():
            attend(own0 + i)
            attend(oth0 + i)

        k = i - lag

        @pl.when(jnp.logical_and(k >= 0, k < half))
        def _():
            chain(k)

        j = i - top_lag - 1

        @pl.when(j >= 0)
        def _():
            finish(own0 + j, e_mine[j])
            carry_copy(j).wait_recv()
            finish(oth0 + j, e_oth[j])

        return c

    lax.fori_loop(0, half + top_lag + 1, step, 0)

    slabs = length // E
    for g in range(slabs):
        ss_loc[pl.ds(g, 1), :] = jnp.sum(acc[pl.ds(g * E, E), :].T, axis=0, keepdims=True)
    for d in range(1, ways):
        norm_copy(d).start()
    for d in range(1, ways):
        norm_copy(d).wait_recv()
    sums = ss_loc[...]
    for d in range(1, ways):
        sums = sums + ss_in[d - 1]
    inverse = lax.rsqrt(sums / (heads_all * E) + EPSILON)
    for g in range(slabs):
        acc[pl.ds(g * E, E), :] = jnp.broadcast_to(inverse[g : g + 1, :], (E, E)).T

    def write(h, c):
        o_buf[h] = (mix[h] * acc[...] * gain[pl.ds(h, 1), :]).astype(BF16)
        store(h).start()
        return c

    lax.fori_loop(0, heads, write, 0)

    def drain(k, c):
        state_copy(k).wait_send()
        chip_copy(k).wait_send()
        carry_copy(k).wait_send()

        @pl.when(z < groups - 1)
        def _():
            chain_copy(k).wait_send()

        store(k).wait()
        store(half + k).wait()
        return c

    lax.fori_loop(0, half, drain, 0)
    for d in range(1, ways):
        norm_copy(d).wait_send()


def body(runs, ways, queries, key_rows, value_rows, decay_rates, out_gain):
    length = queries.shape[0]
    heads = decay_rates.shape[0]
    half = heads // 2
    blocks = length // BLOCK
    dma = pltpu.SemaphoreType.DMA
    states = [pltpu.VMEM((half, E, E), F32)]
    sems = [dma((half,))]
    any_spec = pl.BlockSpec(memory_space=pl.ANY)
    return pl.pallas_call(
        functools.partial(kernel, runs, ways, heads * ways),
        out_shape=jax.ShapeDtypeStruct(queries.shape, BF16),
        in_specs=[any_spec] * 3
        + [pl.BlockSpec(memory_space=pltpu.SMEM), pl.BlockSpec(memory_space=pltpu.VMEM)],
        out_specs=any_spec,
        scratch_shapes=[pltpu.VMEM((heads, length, E), BF16)] * 4
        + [
            pltpu.VMEM((heads, length, E), F32),
            pltpu.VMEM((length, E), F32),
            pltpu.VMEM((heads, blocks - 1, E, E), F32),
            pltpu.VMEM((heads, E, E), F32),
        ]
        + states * 8
        + [pltpu.VMEM((length // E, E), F32), pltpu.VMEM((max(ways - 1, 1), length // E, E), F32)]
        + [dma((heads,))] * 4
        + sems * 8
        + [dma((max(ways - 1, 1),))] * 2,
        compiler_params=pltpu.CompilerParams(
            collective_id=0, has_side_effects=True, vmem_limit_bytes=52 * 1024 * 1024
        ),
        cost_estimate=pl.CostEstimate(
            flops=12 * length * BLOCK * heads * E, bytes_accessed=8 * length * heads * E, transcendentals=0
        ),
    )(queries, key_rows, value_rows, decay_rates, out_gain.reshape(heads, E))


def solution(mesh):
    placed = (P("seq", "head"), P("seq", "head"), P("seq", "head"), P("head"), P("head"))
    return jax.shard_map(
        functools.partial(body, mesh.shape["seq"], mesh.shape["head"]),
        mesh=mesh, in_specs=placed, out_specs=P("seq", "head"), check_vma=False,
    )
```

```python
import functools

import jax
import jax.numpy as jnp
from jax import lax
from jax.experimental import pallas as pl
from jax.experimental.pallas import tpu as pltpu
from jax.sharding import PartitionSpec as P

E = 128
BLOCK = 256
EPSILON = 1e-06
GROUP = 4
F32 = jnp.float32
BF16 = jnp.bfloat16


def dot(a, b, contract):
    return lax.dot_general(a, b, ((contract[:1], contract[1:]), ((), ())), preferred_element_type=F32)


def kernel(
    runs, ways,
    q_hbm, k_hbm, v_hbm, rates_hbm, out_hbm, sums_ref,
    rates, q_buf, k_buf, v_buf, o_buf, mix, acc, entering,
    s_loc, s_oth, c_tot, c_oth, p_in, p_out, e_mine, e_send, e_oth, ss_loc, ss_in,
    r_sem, q_sem, k_sem, v_sem, o_sem, s_ss, s_rs, c_ss, c_rs, p_ss, p_rs, e_ss, e_rs, n_ss, n_rs,
):
    heads, length = q_buf.shape[0], q_buf.shape[1]
    half = heads // 2
    blocks = length // BLOCK
    groups = runs // GROUP
    me = lax.axis_index("seq")
    way = lax.axis_index("head")
    core = lax.rem(me, 2)
    x = lax.rem(me // 2, 2)
    z = me // GROUP
    core_peer = me + 1 - 2 * core
    x_peer = me + 2 - 4 * x
    own0 = core * half
    oth0 = (1 - core) * half
    core_f = core.astype(F32)
    x_f = x.astype(F32)

    def load(hbm, buf, sem, h):
        return pltpu.make_async_copy(hbm.at[:, pl.ds(pl.multiple_of(h * E, E), E)], buf.at[h], sem.at[h])

    def store(h):
        return pltpu.make_async_copy(o_buf.at[h], out_hbm.at[:, pl.ds(pl.multiple_of(h * E, E), E)], o_sem.at[h])

    def remote(src, dst, ss, rs, seq, head):
        return pltpu.make_async_remote_copy(
            src_ref=src, dst_ref=dst, send_sem=ss, recv_sem=rs,
            device_id={"seq": seq, "head": head}, device_id_type=pl.DeviceIdType.MESH,
        )

    def state_copy(k):
        return remote(s_loc.at[oth0 + k], s_oth.at[k], s_ss.at[k], s_rs.at[k], core_peer, way)

    def chip_copy(k):
        return remote(c_tot.at[k], c_oth.at[k], c_ss.at[k], c_rs.at[k], x_peer, way)

    def chain_copy(k):
        up = lax.rem(me + GROUP, runs)
        return remote(p_out.at[k], p_in.at[k], p_ss.at[k], p_rs.at[k], up, way)

    def carry_copy(k):
        return remote(e_send.at[k], e_oth.at[k], e_ss.at[k], e_rs.at[k], core_peer, way)

    def norm_copy(d):
        return remote(ss_loc, ss_in.at[d - 1], n_ss.at[d - 1], n_rs.at[d - 1], me, lax.rem(way + d, ways))

    def start_states(k, c):
        for h in (own0 + k, oth0 + k):
            load(k_hbm, k_buf, k_sem, h).start()
            load(v_hbm, v_buf, v_sem, h).start()
        return c

    def start_queries(k, c):
        for h in (own0 + k, oth0 + k):
            load(q_hbm, q_buf, q_sem, h).start()
        return c

    rates_copy = pltpu.make_async_copy(rates_hbm, rates, r_sem)
    rates_copy.start()
    lax.fori_loop(0, half, start_states, 0)
    lax.fori_loop(0, half, start_queries, 0)

    barrier = pltpu.get_barrier_semaphore()

    def greet(seq, head):
        pl.semaphore_signal(
            barrier, inc=1, device_id={"seq": seq, "head": head}, device_id_type=pl.DeviceIdType.MESH
        )

    greet(core_peer, way)
    greet(x_peer, way)
    for d in range(1, ways):
        greet(me, lax.rem(way + d, ways))

    @pl.when(z > 0)
    def _():
        greet(me - GROUP, way)

    @pl.when(z < groups - 1)
    def _():
        greet(me + GROUP, way)

    @pl.when(z == 0)
    def _():
        p_in[...] = jnp.zeros_like(p_in)

    acc[...] = jnp.zeros_like(acc)
    rates_copy.wait()

    def power(rate, steps):
        return jnp.exp(jnp.full((1, E), -rate * steps, F32))

    row = lax.broadcasted_iota(jnp.int32, (BLOCK, E), 0).astype(F32)

    def local_states(k):
        pair = (oth0 + k, own0 + k)
        for h in pair:
            load(k_hbm, k_buf, k_sem, h).wait()
            load(v_hbm, v_buf, v_sem, h).wait()
        whole = [power(rates[h], float(BLOCK)) for h in pair]
        scale = [jnp.exp(-rates[h] * (BLOCK - 1 - row)) for h in pair]
        state = [None, None]
        for b in range(blocks):
            rows = pl.ds(b * BLOCK, BLOCK)
            for n, h in enumerate(pair):
                scaled = (k_buf[h, rows, :].astype(F32) * scale[n]).astype(BF16)
                part = dot(scaled, v_buf[h, rows, :], (0, 0))
                state[n] = part if b == 0 else state[n] * whole[n] + part
                if b < blocks - 1:
                    entering[h, b] = state[n]
                else:
                    s_loc[h] = state[n]

    def chip_total(k):
        rate = rates[own0 + k]
        state_copy(k).wait_recv()
        mine = power(rate, length * (1.0 - core_f))
        other = power(rate, length * core_f)
        c_tot[k] = mine * s_loc[own0 + k] + other * s_oth[k]
        chip_copy(k).start()

    def state_step(k, c):
        local_states(k)
        state_copy(k).start()
        chip_total(k - 1)
        return c

    local_states(0)
    pl.semaphore_wait(barrier, 2 + (ways - 1) + jnp.minimum(z, 1) + jnp.minimum(groups - 1 - z, 1))
    state_copy(0).start()
    lax.fori_loop(1, half, state_step, 0)
    chip_total(half - 1)

    small = E
    down = lax.broadcasted_iota(jnp.int32, (small, small), 0) - lax.broadcasted_iota(jnp.int32, (small, small), 1)
    down_f = down.astype(F32)

    def attend(k):
        pair = (own0 + k, oth0 + k)
        for h in pair:
            load(q_hbm, q_buf, q_sem, h).wait()
        near = [jnp.where(down >= 0, jnp.exp(-rates[h] * jnp.maximum(down_f, 0.0)), 0.0) for h in pair]
        far = [jnp.exp(-rates[h] * (down_f + small)) for h in pair]
        units = [(n, b) for n in range(2) for b in range(blocks)]

        def score(unit):
            rows = pl.ds(unit[1] * BLOCK, BLOCK)
            return dot(q_buf[pair[unit[0]], rows, :], k_buf[pair[unit[0]], rows, :], (1, 1))

        ahead = score(units[0])
        for at, (n, b) in enumerate(units):
            scores = ahead
            if at + 1 < len(units):
                ahead = score(units[at + 1])
            vals = v_buf[pair[n], pl.ds(b * BLOCK, BLOCK), :]
            top = (scores[:small, :small] * near[n]).astype(BF16)
            low = jnp.concatenate(
                [(scores[small:, :small] * far[n]).astype(BF16), (scores[small:, small:] * near[n]).astype(BF16)],
                axis=1,
            )
            mix[pair[n], pl.ds(b * BLOCK, small), :] = dot(top, vals[:small], (1, 0))
            mix[pair[n], pl.ds(b * BLOCK + small, small), :] = dot(low, vals, (1, 0))

    def chain(k):
        rate = rates[own0 + k]
        chip_copy(k).wait_recv()

        @pl.when(z > 0)
        def _():
            chain_copy(k).wait_recv()

        before = p_in[k]
        other = c_oth[k]
        two = 2.0 * length

        @pl.when(z < groups - 1)
        def _():
            total = power(rate, two * (1.0 - x_f)) * c_tot[k] + power(rate, two * x_f) * other
            p_out[k] = power(rate, 2.0 * two) * before + total
            chain_copy(k).start()

        chip = power(rate, two * x_f) * before + x_f * other

        @pl.when(core == 0)
        def _():
            e_mine[k] = chip
            e_send[k] = power(rate, float(length)) * chip + s_loc[own0 + k]

        @pl.when(core == 1)
        def _():
            e_mine[k] = power(rate, float(length)) * chip + s_oth[k]
            e_send[k] = chip

        carry_copy(k).start()

    def finish(k):
        pair = (own0 + k, oth0 + k)
        carry_copy(k).wait_recv()
        carry = (e_mine[k], e_oth[k])
        scale = [jnp.exp(-rates[h] * (row + 1.0)) for h in pair]
        for b in range(blocks):
            rows = pl.ds(b * BLOCK, BLOCK)
            squares = acc[rows, :]
            for n, h in enumerate(pair):
                state = carry[n]
                if b > 0:
                    state = power(rates[h], float(b * BLOCK)) * state + entering[h, b - 1]
                mixed = mix[h, rows, :] + scale[n] * dot(q_buf[h, rows, :], state.astype(BF16), (1, 0))
                o_buf[h, rows, :] = mixed.astype(BF16)
                squares = squares + mixed * mixed
            acc[rows, :] = squares
        for h in pair:
            store(h).start()

    top_lag = min((3 * (groups - 1) + 1) // 2, half)
    lag = jnp.minimum((3 * z + 1) // 2, half)

    def step(i, c):
        @pl.when(i < half)
        def _():
            attend(i)

        def turn(n, c):
            k = 2 * (i - lag) + n

            @pl.when(jnp.logical_and(k >= 0, k < half))
            def _():
                chain(k)

            j = 2 * (i - top_lag) + n - 1

            @pl.when(jnp.logical_and(j >= 0, j < half))
            def _():
                finish(j)

            return c

        return lax.fori_loop(0, 2, turn, c)

    lax.fori_loop(0, max(half, top_lag + half // 2 + 1), step, 0)

    slabs = length // E
    for g in range(slabs):
        ss_loc[pl.ds(g, 1), :] = jnp.sum(acc[pl.ds(g * E, E), :].T, axis=0, keepdims=True)
    for d in range(1, ways):
        norm_copy(d).start()
    for d in range(1, ways):
        norm_copy(d).wait_recv()
    sums = ss_loc[...]
    for d in range(1, ways):
        sums = sums + ss_in[d - 1]
    sums_ref[...] = sums

    def drain(k, c):
        state_copy(k).wait_send()
        chip_copy(k).wait_send()
        carry_copy(k).wait_send()

        @pl.when(z < groups - 1)
        def _():
            chain_copy(k).wait_send()

        store(k).wait()
        store(half + k).wait()
        return c

    lax.fori_loop(0, half, drain, 0)
    for d in range(1, ways):
        norm_copy(d).wait_send()


def normalise(width, mixed_ref, sums_ref, gain_ref, out_ref):
    slabs = mixed_ref.shape[0] // E
    for t in range(slabs):
        sums = sums_ref[pl.ds(pl.program_id(0) * slabs + t, 1), :]
        inverse = jnp.broadcast_to(lax.rsqrt(sums / width + EPSILON), (E, E)).T
        rows = pl.ds(t * E, E)
        for h in range(mixed_ref.shape[1] // E):
            cols = pl.ds(h * E, E)
            out_ref[rows, cols] = (mixed_ref[rows, cols].astype(F32) * inverse * gain_ref[:, cols]).astype(BF16)


def body(runs, ways, queries, key_rows, value_rows, decay_rates, out_gain):
    length, columns = queries.shape
    heads = decay_rates.shape[0]
    half = heads // 2
    blocks = length // BLOCK
    dma = pltpu.SemaphoreType.DMA
    states = [pltpu.VMEM((half, E, E), F32)]
    sems = [dma((half,))]
    any_spec = pl.BlockSpec(memory_space=pl.ANY)
    sums_shape = (length // E, E)
    mixed, sums = pl.pallas_call(
        functools.partial(kernel, runs, ways),
        out_shape=(jax.ShapeDtypeStruct(queries.shape, BF16), jax.ShapeDtypeStruct(sums_shape, F32)),
        in_specs=[pl.BlockSpec(memory_space=pltpu.HBM)] * 4,
        out_specs=(any_spec, pl.BlockSpec(memory_space=pltpu.VMEM)),
        scratch_shapes=[pltpu.SMEM((heads,), F32)]
        + [pltpu.VMEM((heads, length, E), BF16)] * 4
        + [
            pltpu.VMEM((heads, length, E), F32),
            pltpu.VMEM((length, E), F32),
            pltpu.VMEM((heads, blocks - 1, E, E), F32),
            pltpu.VMEM((heads, E, E), F32),
        ]
        + states * 8
        + [pltpu.VMEM(sums_shape, F32), pltpu.VMEM((max(ways - 1, 1),) + sums_shape, F32)]
        + [dma]
        + [dma((heads,))] * 4
        + sems * 8
        + [dma((max(ways - 1, 1),))] * 2,
        compiler_params=pltpu.CompilerParams(
            collective_id=0, has_side_effects=True, vmem_limit_bytes=44 * 1024 * 1024
        ),
        cost_estimate=pl.CostEstimate(
            flops=12 * length * BLOCK * heads * E, bytes_accessed=8 * length * heads * E, transcendentals=0
        ),
    )(queries, key_rows, value_rows, decay_rates)
    tile = BLOCK
    return pl.pallas_call(
        functools.partial(normalise, float(heads * ways * E)),
        out_shape=jax.ShapeDtypeStruct(queries.shape, BF16),
        grid=(length // tile,),
        in_specs=[
            pl.BlockSpec((tile, columns), lambda i: (i, 0)),
            pl.BlockSpec(sums_shape, lambda i: (0, 0)),
            pl.BlockSpec((1, columns), lambda i: (0, 0)),
        ],
        out_specs=pl.BlockSpec((tile, columns), lambda i: (i, 0)),
        cost_estimate=pl.CostEstimate(
            flops=3 * length * columns, bytes_accessed=4 * length * columns, transcendentals=0
        ),
    )(mixed, sums, out_gain.reshape(1, columns))


def solution(mesh):
    placed = (P("seq", "head"), P("seq", "head"), P("seq", "head"), P("head"), P("head"))
    return jax.shard_map(
        functools.partial(body, mesh.shape["seq"], mesh.shape["head"]),
        mesh=mesh, in_specs=placed, out_specs=P("seq", "head"), check_vma=False,
    )
```

```python
import functools

import jax
import jax.numpy as jnp
from jax import lax
from jax.experimental import pallas as pl
from jax.experimental.pallas import tpu as pltpu
from jax.sharding import PartitionSpec as P

E = 128
BLOCK = 256
EPSILON = 1e-06
GROUP = 4
F32 = jnp.float32
BF16 = jnp.bfloat16


def dot(a, b, contract):
    return lax.dot_general(a, b, ((contract[:1], contract[1:]), ((), ())), preferred_element_type=F32)


def kernel(
    runs, ways,
    q_hbm, k_hbm, v_hbm, rates_hbm, mix, sums_ref,
    rates, q_buf, k_buf, v_buf, acc, entering,
    s_loc, s_oth, c_tot, c_oth, p_in, p_out, e_mine, e_send, e_oth, ss_loc, ss_in,
    r_sem, q_sem, k_sem, v_sem, s_ss, s_rs, c_ss, c_rs, p_ss, p_rs, e_ss, e_rs, n_ss, n_rs,
):
    heads, length = q_buf.shape[0], q_buf.shape[1]
    half = heads // 2
    blocks = length // BLOCK
    groups = runs // GROUP
    me = lax.axis_index("seq")
    way = lax.axis_index("head")
    core = lax.rem(me, 2)
    x = lax.rem(me // 2, 2)
    z = me // GROUP
    core_peer = me + 1 - 2 * core
    x_peer = me + 2 - 4 * x
    own0 = core * half
    oth0 = (1 - core) * half
    core_f = core.astype(F32)
    x_f = x.astype(F32)

    def load(hbm, buf, sem, h):
        return pltpu.make_async_copy(hbm.at[:, pl.ds(pl.multiple_of(h * E, E), E)], buf.at[h], sem.at[h])

    def remote(src, dst, ss, rs, seq, head):
        return pltpu.make_async_remote_copy(
            src_ref=src, dst_ref=dst, send_sem=ss, recv_sem=rs,
            device_id={"seq": seq, "head": head}, device_id_type=pl.DeviceIdType.MESH,
        )

    def state_copy(k):
        return remote(s_loc.at[oth0 + k], s_oth.at[k], s_ss.at[k], s_rs.at[k], core_peer, way)

    def chip_copy(k):
        return remote(c_tot.at[k], c_oth.at[k], c_ss.at[k], c_rs.at[k], x_peer, way)

    def chain_copy(k):
        up = lax.rem(me + GROUP, runs)
        return remote(p_out.at[k], p_in.at[k], p_ss.at[k], p_rs.at[k], up, way)

    def carry_copy(k):
        return remote(e_send.at[k], e_oth.at[k], e_ss.at[k], e_rs.at[k], core_peer, way)

    def norm_copy(d):
        return remote(ss_loc, ss_in.at[d - 1], n_ss.at[d - 1], n_rs.at[d - 1], me, lax.rem(way + d, ways))

    def start_states(k, c):
        for h in (own0 + k, oth0 + k):
            load(k_hbm, k_buf, k_sem, h).start()
            load(v_hbm, v_buf, v_sem, h).start()
        return c

    def start_queries(k, c):
        for h in (own0 + k, oth0 + k):
            load(q_hbm, q_buf, q_sem, h).start()
        return c

    rates_copy = pltpu.make_async_copy(rates_hbm, rates, r_sem)
    rates_copy.start()
    lax.fori_loop(0, half, start_states, 0)
    lax.fori_loop(0, half, start_queries, 0)

    barrier = pltpu.get_barrier_semaphore()

    def greet(seq, head):
        pl.semaphore_signal(
            barrier, inc=1, device_id={"seq": seq, "head": head}, device_id_type=pl.DeviceIdType.MESH
        )

    greet(core_peer, way)
    greet(x_peer, way)
    for d in range(1, ways):
        greet(me, lax.rem(way + d, ways))

    @pl.when(z > 0)
    def _():
        greet(me - GROUP, way)

    @pl.when(z < groups - 1)
    def _():
        greet(me + GROUP, way)

    @pl.when(z == 0)
    def _():
        p_in[...] = jnp.zeros_like(p_in)

    acc[...] = jnp.zeros_like(acc)
    rates_copy.wait()

    def power(rate, steps):
        return jnp.exp(jnp.full((1, E), -rate * steps, F32))

    row = lax.broadcasted_iota(jnp.int32, (BLOCK, E), 0).astype(F32)

    def local_states(k):
        pair = (oth0 + k, own0 + k)
        for h in pair:
            load(k_hbm, k_buf, k_sem, h).wait()
            load(v_hbm, v_buf, v_sem, h).wait()
        whole = [power(rates[h], float(BLOCK)) for h in pair]
        scale = [jnp.exp(-rates[h] * (BLOCK - 1 - row)) for h in pair]
        state = [None, None]
        for b in range(blocks):
            rows = pl.ds(b * BLOCK, BLOCK)
            for n, h in enumerate(pair):
                scaled = (k_buf[h, rows, :].astype(F32) * scale[n]).astype(BF16)
                part = dot(scaled, v_buf[h, rows, :], (0, 0))
                state[n] = part if b == 0 else state[n] * whole[n] + part
                if b < blocks - 1:
                    entering[h, b] = state[n]
                else:
                    s_loc[h] = state[n]

    def chip_total(k):
        rate = rates[own0 + k]
        state_copy(k).wait_recv()
        mine = power(rate, length * (1.0 - core_f))
        other = power(rate, length * core_f)
        c_tot[k] = mine * s_loc[own0 + k] + other * s_oth[k]
        chip_copy(k).start()

    def state_step(k, c):
        local_states(k)
        state_copy(k).start()
        chip_total(k - 1)
        return c

    local_states(0)
    pl.semaphore_wait(barrier, 2 + (ways - 1) + jnp.minimum(z, 1) + jnp.minimum(groups - 1 - z, 1))
    state_copy(0).start()
    lax.fori_loop(1, half, state_step, 0)
    chip_total(half - 1)

    small = E
    down = lax.broadcasted_iota(jnp.int32, (small, small), 0) - lax.broadcasted_iota(jnp.int32, (small, small), 1)
    down_f = down.astype(F32)

    def attend(k):
        pair = (own0 + k, oth0 + k)
        for h in pair:
            load(q_hbm, q_buf, q_sem, h).wait()
        near = [jnp.where(down >= 0, jnp.exp(-rates[h] * jnp.maximum(down_f, 0.0)), 0.0) for h in pair]
        far = [jnp.exp(-rates[h] * (down_f + small)) for h in pair]
        units = [(n, b) for n in range(2) for b in range(blocks)]

        def score(unit):
            rows = pl.ds(unit[1] * BLOCK, BLOCK)
            return dot(q_buf[pair[unit[0]], rows, :], k_buf[pair[unit[0]], rows, :], (1, 1))

        ahead = score(units[0])
        for at, (n, b) in enumerate(units):
            scores = ahead
            if at + 1 < len(units):
                ahead = score(units[at + 1])
            vals = v_buf[pair[n], pl.ds(b * BLOCK, BLOCK), :]
            top = (scores[:small, :small] * near[n]).astype(BF16)
            low = jnp.concatenate(
                [(scores[small:, :small] * far[n]).astype(BF16), (scores[small:, small:] * near[n]).astype(BF16)],
                axis=1,
            )
            mix[pair[n], pl.ds(b * BLOCK, small), :] = dot(top, vals[:small], (1, 0))
            mix[pair[n], pl.ds(b * BLOCK + small, small), :] = dot(low, vals, (1, 0))

    def chain(k):
        rate = rates[own0 + k]
        chip_copy(k).wait_recv()

        @pl.when(z > 0)
        def _():
            chain_copy(k).wait_recv()

        before = p_in[k]
        other = c_oth[k]
        two = 2.0 * length

        @pl.when(z < groups - 1)
        def _():
            total = power(rate, two * (1.0 - x_f)) * c_tot[k] + power(rate, two * x_f) * other
            p_out[k] = power(rate, 2.0 * two) * before + total
            chain_copy(k).start()

        chip = power(rate, two * x_f) * before + x_f * other

        @pl.when(core == 0)
        def _():
            e_mine[k] = chip
            e_send[k] = power(rate, float(length)) * chip + s_loc[own0 + k]

        @pl.when(core == 1)
        def _():
            e_mine[k] = power(rate, float(length)) * chip + s_oth[k]
            e_send[k] = chip

        carry_copy(k).start()

    def finish(k):
        pair = (own0 + k, oth0 + k)
        carry_copy(k).wait_recv()
        carry = (e_mine[k], e_oth[k])
        scale = [jnp.exp(-rates[h] * (row + 1.0)) for h in pair]
        for b in range(blocks):
            rows = pl.ds(b * BLOCK, BLOCK)
            squares = acc[rows, :]
            for n, h in enumerate(pair):
                state = carry[n]
                if b > 0:
                    state = power(rates[h], float(b * BLOCK)) * state + entering[h, b - 1]
                mixed = mix[h, rows, :] + scale[n] * dot(q_buf[h, rows, :], state.astype(BF16), (1, 0))
                mix[h, rows, :] = mixed
                squares = squares + mixed * mixed
            acc[rows, :] = squares

    top_lag = min((3 * (groups - 1) + 1) // 2, half)
    lag = jnp.minimum((3 * z + 1) // 2, half)

    def step(i, c):
        @pl.when(i < half)
        def _():
            attend(i)

        def turn(n, c):
            k = 2 * (i - lag) + n

            @pl.when(jnp.logical_and(k >= 0, k < half))
            def _():
                chain(k)

            j = 2 * (i - top_lag) + n - 1

            @pl.when(jnp.logical_and(j >= 0, j < half))
            def _():
                finish(j)

            return c

        return lax.fori_loop(0, 2, turn, c)

    lax.fori_loop(0, max(half, top_lag + half // 2 + 1), step, 0)

    slabs = length // E
    for g in range(slabs):
        ss_loc[pl.ds(g, 1), :] = jnp.sum(acc[pl.ds(g * E, E), :].T, axis=0, keepdims=True)
    for d in range(1, ways):
        norm_copy(d).start()
    for d in range(1, ways):
        norm_copy(d).wait_recv()
    sums = ss_loc[...]
    for d in range(1, ways):
        sums = sums + ss_in[d - 1]
    sums_ref[...] = sums

    def drain(k, c):
        state_copy(k).wait_send()
        chip_copy(k).wait_send()
        carry_copy(k).wait_send()

        @pl.when(z < groups - 1)
        def _():
            chain_copy(k).wait_send()

        return c

    lax.fori_loop(0, half, drain, 0)
    for d in range(1, ways):
        norm_copy(d).wait_send()


def normalise(width, mixed_ref, sums_ref, gain_ref, out_ref):
    slabs = mixed_ref.shape[1] // E
    for t in range(slabs):
        sums = sums_ref[pl.ds(pl.program_id(0) * slabs + t, 1), :]
        inverse = jnp.broadcast_to(lax.rsqrt(sums / width + EPSILON), (E, E)).T
        rows = pl.ds(t * E, E)
        for h in range(mixed_ref.shape[0]):
            cols = pl.ds(h * E, E)
            out_ref[rows, cols] = (mixed_ref[h, rows, :] * inverse * gain_ref[:, cols]).astype(BF16)


def body(runs, ways, queries, key_rows, value_rows, decay_rates, out_gain):
    length, columns = queries.shape
    heads = decay_rates.shape[0]
    half = heads // 2
    blocks = length // BLOCK
    dma = pltpu.SemaphoreType.DMA
    states = [pltpu.VMEM((half, E, E), F32)]
    sems = [dma((half,))]
    fixed = [pltpu.with_memory_space_constraint(a, pltpu.HBM) for a in (queries, key_rows, value_rows, decay_rates)]
    gain = pltpu.with_memory_space_constraint(out_gain.reshape(1, columns), pltpu.HBM)
    sums_shape = (length // E, E)
    mixed, sums = pl.pallas_call(
        functools.partial(kernel, runs, ways),
        out_shape=(jax.ShapeDtypeStruct((heads, length, E), F32), jax.ShapeDtypeStruct(sums_shape, F32)),
        in_specs=[pl.BlockSpec(memory_space=pltpu.HBM)] * 4,
        out_specs=(pl.BlockSpec(memory_space=pltpu.VMEM),) * 2,
        scratch_shapes=[pltpu.SMEM((heads,), F32)]
        + [pltpu.VMEM((heads, length, E), BF16)] * 3
        + [
            pltpu.VMEM((length, E), F32),
            pltpu.VMEM((heads, blocks - 1, E, E), F32),
            pltpu.VMEM((heads, E, E), F32),
        ]
        + states * 8
        + [pltpu.VMEM(sums_shape, F32), pltpu.VMEM((max(ways - 1, 1),) + sums_shape, F32)]
        + [dma]
        + [dma((heads,))] * 3
        + sems * 8
        + [dma((max(ways - 1, 1),))] * 2,
        compiler_params=pltpu.CompilerParams(
            collective_id=0, has_side_effects=True, vmem_limit_bytes=40 * 1024 * 1024
        ),
        cost_estimate=pl.CostEstimate(
            flops=12 * length * BLOCK * heads * E, bytes_accessed=8 * length * heads * E, transcendentals=0
        ),
    )(*fixed)
    tile = BLOCK
    return pl.pallas_call(
        functools.partial(normalise, float(heads * ways * E)),
        out_shape=jax.ShapeDtypeStruct(queries.shape, BF16),
        grid=(length // tile,),
        in_specs=[
            pl.BlockSpec((heads, tile, E), lambda i: (0, i, 0)),
            pl.BlockSpec(sums_shape, lambda i: (0, 0)),
            pl.BlockSpec((1, columns), lambda i: (0, 0)),
        ],
        out_specs=pl.BlockSpec((tile, columns), lambda i: (i, 0)),
        compiler_params=pltpu.CompilerParams(vmem_limit_bytes=16 * 1024 * 1024),
        cost_estimate=pl.CostEstimate(
            flops=3 * length * columns, bytes_accessed=4 * length * columns, transcendentals=0
        ),
    )(mixed, sums, gain)


def solution(mesh):
    placed = (P("seq", "head"), P("seq", "head"), P("seq", "head"), P("head"), P("head"))
    return jax.shard_map(
        functools.partial(body, mesh.shape["seq"], mesh.shape["head"]),
        mesh=mesh, in_specs=placed, out_specs=P("seq", "head"), check_vma=False,
    )
```

```python
import functools

import jax
import jax.numpy as jnp
from jax import lax
from jax.experimental import pallas as pl
from jax.experimental.pallas import tpu as pltpu
from jax.sharding import PartitionSpec as P

E = 128
BLOCK = 256
EPSILON = 1e-06
GROUP = 4
F32 = jnp.float32
BF16 = jnp.bfloat16


def dot(a, b, contract):
    return lax.dot_general(a, b, ((contract[:1], contract[1:]), ((), ())), preferred_element_type=F32)


def kernel(
    runs, ways,
    q_hbm, k_hbm, v_hbm, rates_hbm, mix, sums_ref,
    rates, q_buf, k_buf, v_buf, acc, entering,
    s_loc, s_oth, c_tot, c_oth, p_in, p_out, e_mine, e_send, e_oth, ss_loc, ss_in,
    r_sem, q_sem, k_sem, v_sem, s_ss, s_rs, c_ss, c_rs, p_ss, p_rs, e_ss, e_rs, n_ss, n_rs,
):
    heads, length = q_buf.shape[0], q_buf.shape[1]
    half = heads // 2
    blocks = length // BLOCK
    groups = runs // GROUP
    me = lax.axis_index("seq")
    way = lax.axis_index("head")
    core = lax.rem(me, 2)
    x = lax.rem(me // 2, 2)
    z = me // GROUP
    core_peer = me + 1 - 2 * core
    x_peer = me + 2 - 4 * x
    own0 = core * half
    oth0 = (1 - core) * half
    core_f = core.astype(F32)
    x_f = x.astype(F32)

    def load(hbm, buf, sem, h):
        return pltpu.make_async_copy(hbm.at[:, pl.ds(pl.multiple_of(h * E, E), E)], buf.at[h], sem.at[h])

    def remote(src, dst, ss, rs, seq, head):
        return pltpu.make_async_remote_copy(
            src_ref=src, dst_ref=dst, send_sem=ss, recv_sem=rs,
            device_id={"seq": seq, "head": head}, device_id_type=pl.DeviceIdType.MESH,
        )

    def state_copy(k):
        return remote(s_loc.at[oth0 + k], s_oth.at[k], s_ss.at[k], s_rs.at[k], core_peer, way)

    def chip_copy(k):
        return remote(c_tot.at[k], c_oth.at[k], c_ss.at[k], c_rs.at[k], x_peer, way)

    def chain_copy(k):
        up = lax.rem(me + GROUP, runs)
        return remote(p_out.at[k], p_in.at[k], p_ss.at[k], p_rs.at[k], up, way)

    def carry_copy(k):
        return remote(e_send.at[k], e_oth.at[k], e_ss.at[k], e_rs.at[k], core_peer, way)

    def norm_copy(d):
        return remote(ss_loc, ss_in.at[d - 1], n_ss.at[d - 1], n_rs.at[d - 1], me, lax.rem(way + d, ways))

    def start_states(k, c):
        for h in (own0 + k, oth0 + k):
            load(k_hbm, k_buf, k_sem, h).start()
            load(v_hbm, v_buf, v_sem, h).start()
        return c

    def start_queries(k, c):
        for h in (own0 + k, oth0 + k):
            load(q_hbm, q_buf, q_sem, h).start()
        return c

    rates_copy = pltpu.make_async_copy(rates_hbm, rates, r_sem)
    rates_copy.start()
    lax.fori_loop(0, half, start_states, 0)
    lax.fori_loop(0, half, start_queries, 0)

    barrier = pltpu.get_barrier_semaphore()

    def greet(seq, head):
        pl.semaphore_signal(
            barrier, inc=1, device_id={"seq": seq, "head": head}, device_id_type=pl.DeviceIdType.MESH
        )

    greet(core_peer, way)
    greet(x_peer, way)
    for d in range(1, ways):
        greet(me, lax.rem(way + d, ways))

    @pl.when(z > 0)
    def _():
        greet(me - GROUP, way)

    @pl.when(z < groups - 1)
    def _():
        greet(me + GROUP, way)

    @pl.when(z == 0)
    def _():
        p_in[...] = jnp.zeros_like(p_in)

    acc[...] = jnp.zeros_like(acc)
    rates_copy.wait()

    def power(rate, steps):
        return jnp.exp(jnp.full((1, E), -rate * steps, F32))

    row = lax.broadcasted_iota(jnp.int32, (8, E), 0).astype(F32)

    def rising(rate):
        column = jnp.exp(-rate * (row + 1.0))
        while column.shape[0] < BLOCK:
            column = jnp.concatenate([column, column * power(rate, float(column.shape[0]))], axis=0)
        return column

    def falling(rate):
        column = jnp.exp(-rate * (7.0 - row))
        while column.shape[0] < BLOCK:
            column = jnp.concatenate([column * power(rate, float(column.shape[0])), column], axis=0)
        return column


    def local_states(k):
        pair = (oth0 + k, own0 + k)
        for h in pair:
            load(k_hbm, k_buf, k_sem, h).wait()
            load(v_hbm, v_buf, v_sem, h).wait()
        whole = [power(rates[h], float(BLOCK)) for h in pair]
        scale = [falling(rates[h]) for h in pair]
        state = [None, None]
        for b in range(blocks):
            rows = pl.ds(b * BLOCK, BLOCK)
            for n, h in enumerate(pair):
                scaled = (k_buf[h, rows, :].astype(F32) * scale[n]).astype(BF16)
                part = dot(scaled, v_buf[h, rows, :], (0, 0))
                state[n] = part if b == 0 else state[n] * whole[n] + part
                if b < blocks - 1:
                    entering[h, b] = state[n]
                else:
                    s_loc[h] = state[n]

    def chip_total(k):
        rate = rates[own0 + k]
        state_copy(k).wait_recv()
        mine = power(rate, length * (1.0 - core_f))
        other = power(rate, length * core_f)
        c_tot[k] = mine * s_loc[own0 + k] + other * s_oth[k]
        chip_copy(k).start()

    def state_step(k, c):
        local_states(k)
        state_copy(k).start()
        chip_total(k - 1)
        return c

    local_states(0)
    pl.semaphore_wait(barrier, 2 + (ways - 1) + jnp.minimum(z, 1) + jnp.minimum(groups - 1 - z, 1))
    state_copy(0).start()
    lax.fori_loop(1, half, state_step, 0)
    chip_total(half - 1)

    small = E
    down = lax.broadcasted_iota(jnp.int32, (small, small), 0) - lax.broadcasted_iota(jnp.int32, (small, small), 1)
    down_f = down.astype(F32)
    left = (small - 1) - lax.broadcasted_iota(jnp.int32, (1, small), 1).astype(F32)
    blank = jnp.zeros((small, small), BF16)

    def attend(k):
        pair = (own0 + k, oth0 + k)
        for h in pair:
            load(q_hbm, q_buf, q_sem, h).wait()
        near = [jnp.where(down >= 0, jnp.exp(-rates[h] * jnp.maximum(down_f, 0.0)), 0.0) for h in pair]
        far = [rising(rates[h])[:small] * jnp.exp(-rates[h] * left) for h in pair]
        units = [(n, b) for n in range(2) for b in range(blocks)]

        def score(unit):
            rows = pl.ds(unit[1] * BLOCK, BLOCK)
            return dot(q_buf[pair[unit[0]], rows, :], k_buf[pair[unit[0]], rows, :], (1, 1))

        ahead = score(units[0])
        for at, (n, b) in enumerate(units):
            scores = ahead
            if at + 1 < len(units):
                ahead = score(units[at + 1])
            vals = v_buf[pair[n], pl.ds(b * BLOCK, BLOCK), :]
            top = jnp.concatenate([(scores[:small, :small] * near[n]).astype(BF16), blank], axis=1)
            low = jnp.concatenate(
                [(scores[small:, :small] * far[n]).astype(BF16), (scores[small:, small:] * near[n]).astype(BF16)],
                axis=1,
            )
            mix[pair[n], pl.ds(b * BLOCK, BLOCK), :] = dot(jnp.concatenate([top, low], axis=0), vals, (1, 0))

    def chain(k):
        rate = rates[own0 + k]
        chip_copy(k).wait_recv()

        @pl.when(z > 0)
        def _():
            chain_copy(k).wait_recv()

        before = p_in[k]
        other = c_oth[k]
        two = 2.0 * length

        @pl.when(z < groups - 1)
        def _():
            total = power(rate, two * (1.0 - x_f)) * c_tot[k] + power(rate, two * x_f) * other
            p_out[k] = power(rate, 2.0 * two) * before + total
            chain_copy(k).start()

        chip = power(rate, two * x_f) * before + x_f * other

        @pl.when(core == 0)
        def _():
            e_mine[k] = chip
            e_send[k] = power(rate, float(length)) * chip + s_loc[own0 + k]

        @pl.when(core == 1)
        def _():
            e_mine[k] = power(rate, float(length)) * chip + s_oth[k]
            e_send[k] = chip

        carry_copy(k).start()

    def finish(k):
        pair = (own0 + k, oth0 + k)
        carry_copy(k).wait_recv()
        carry = (e_mine[k], e_oth[k])
        scale = [rising(rates[h]) for h in pair]
        for b in range(blocks):
            rows = pl.ds(b * BLOCK, BLOCK)
            squares = acc[rows, :]
            for n, h in enumerate(pair):
                state = carry[n]
                if b > 0:
                    state = power(rates[h], float(b * BLOCK)) * state + entering[h, b - 1]
                mixed = mix[h, rows, :] + scale[n] * dot(q_buf[h, rows, :], state.astype(BF16), (1, 0))
                mix[h, rows, :] = mixed
                squares = squares + mixed * mixed
            acc[rows, :] = squares

    top_lag = min((3 * (groups - 1) + 1) // 2, half)
    lag = jnp.minimum((3 * z + 1) // 2, half)

    def step(i, c):
        @pl.when(i < half)
        def _():
            attend(i)

        def turn(n, c):
            k = 2 * (i - lag) + n

            @pl.when(jnp.logical_and(k >= 0, k < half))
            def _():
                chain(k)

            j = 2 * (i - top_lag) + n - 1

            @pl.when(jnp.logical_and(j >= 0, j < half))
            def _():
                finish(j)

            return c

        return lax.fori_loop(0, 2, turn, c)

    lax.fori_loop(0, max(half, top_lag + half // 2 + 1), step, 0)

    slabs = length // E
    for g in range(slabs):
        ss_loc[pl.ds(g, 1), :] = jnp.sum(acc[pl.ds(g * E, E), :].T, axis=0, keepdims=True)
    for d in range(1, ways):
        norm_copy(d).start()
    for d in range(1, ways):
        norm_copy(d).wait_recv()
    sums = ss_loc[...]
    for d in range(1, ways):
        sums = sums + ss_in[d - 1]
    sums_ref[...] = sums

    def drain(k, c):
        state_copy(k).wait_send()
        chip_copy(k).wait_send()
        carry_copy(k).wait_send()

        @pl.when(z < groups - 1)
        def _():
            chain_copy(k).wait_send()

        return c

    lax.fori_loop(0, half, drain, 0)
    for d in range(1, ways):
        norm_copy(d).wait_send()


def normalise(width, mixed_ref, sums_ref, gain_hbm, out_hbm, gain, ready, gain_sem, out_sem):
    slabs = mixed_ref.shape[1] // E
    fetch = pltpu.make_async_copy(gain_hbm, gain, gain_sem)
    fetch.start()

    def put(t):
        rows = pl.ds(pl.multiple_of(t * E, E), E)
        return pltpu.make_async_copy(ready.at[rows], out_hbm.at[rows], out_sem.at[t])

    fetch.wait()

    def slab(t, c):
        inverse = jnp.broadcast_to(lax.rsqrt(sums_ref[pl.ds(t, 1), :] / width + EPSILON), (E, E)).T
        rows = pl.ds(pl.multiple_of(t * E, E), E)
        for h in range(mixed_ref.shape[0]):
            cols = pl.ds(h * E, E)
            ready[rows, cols] = (mixed_ref[h, rows, :] * inverse * gain[:, cols]).astype(BF16)
        put(t).start()
        return c

    lax.fori_loop(0, slabs, slab, 0)

    def drain(t, c):
        put(t).wait()
        return c

    lax.fori_loop(0, slabs, drain, 0)


def body(runs, ways, queries, key_rows, value_rows, decay_rates, out_gain):
    length, columns = queries.shape
    heads = decay_rates.shape[0]
    half = heads // 2
    blocks = length // BLOCK
    dma = pltpu.SemaphoreType.DMA
    states = [pltpu.VMEM((half, E, E), F32)]
    sems = [dma((half,))]
    fixed = [pltpu.with_memory_space_constraint(a, pltpu.HBM) for a in (queries, key_rows, value_rows, decay_rates)]
    gain = pltpu.with_memory_space_constraint(out_gain.reshape(1, columns), pltpu.HBM)
    sums_shape = (length // E, E)
    mixed, sums = pl.pallas_call(
        functools.partial(kernel, runs, ways),
        out_shape=(jax.ShapeDtypeStruct((heads, length, E), F32), jax.ShapeDtypeStruct(sums_shape, F32)),
        in_specs=[pl.BlockSpec(memory_space=pltpu.HBM)] * 4,
        out_specs=(pl.BlockSpec(memory_space=pltpu.VMEM),) * 2,
        scratch_shapes=[pltpu.SMEM((heads,), F32)]
        + [pltpu.VMEM((heads, length, E), BF16)] * 3
        + [
            pltpu.VMEM((length, E), F32),
            pltpu.VMEM((heads, blocks - 1, E, E), F32),
            pltpu.VMEM((heads, E, E), F32),
        ]
        + states * 8
        + [pltpu.VMEM(sums_shape, F32), pltpu.VMEM((max(ways - 1, 1),) + sums_shape, F32)]
        + [dma]
        + [dma((heads,))] * 3
        + sems * 8
        + [dma((max(ways - 1, 1),))] * 2,
        compiler_params=pltpu.CompilerParams(
            collective_id=0, has_side_effects=True, vmem_limit_bytes=40 * 1024 * 1024
        ),
        cost_estimate=pl.CostEstimate(
            flops=12 * length * BLOCK * heads * E, bytes_accessed=8 * length * heads * E, transcendentals=0
        ),
    )(*fixed)
    return pl.pallas_call(
        functools.partial(normalise, float(heads * ways * E)),
        out_shape=jax.ShapeDtypeStruct(queries.shape, BF16),
        in_specs=[pl.BlockSpec(memory_space=pltpu.VMEM)] * 2 + [pl.BlockSpec(memory_space=pltpu.HBM)],
        out_specs=pl.BlockSpec(memory_space=pltpu.HBM),
        scratch_shapes=[
            pltpu.VMEM((1, columns), F32),
            pltpu.VMEM(queries.shape, BF16),
            dma,
            dma((length // E,)),
        ],
        compiler_params=pltpu.CompilerParams(vmem_limit_bytes=16 * 1024 * 1024),
        cost_estimate=pl.CostEstimate(
            flops=3 * length * columns, bytes_accessed=4 * length * columns, transcendentals=0
        ),
    )(mixed, sums, gain)


def solution(mesh):
    placed = (P("seq", "head"), P("seq", "head"), P("seq", "head"), P("head"), P("head"))
    return jax.shard_map(
        functools.partial(body, mesh.shape["seq"], mesh.shape["head"]),
        mesh=mesh, in_specs=placed, out_specs=P("seq", "head"), check_vma=False,
    )
```

```python
import functools

import jax
import jax.numpy as jnp
from jax import lax
from jax.experimental import pallas as pl
from jax.experimental.pallas import tpu as pltpu
from jax.sharding import PartitionSpec as P

E = 128
BLOCK = 256
EPSILON = 1e-06
GROUP = 4
CUTS = 2
PIECE = E // CUTS
F32 = jnp.float32
BF16 = jnp.bfloat16


def dot(a, b, contract):
    return lax.dot_general(a, b, ((contract[:1], contract[1:]), ((), ())), preferred_element_type=F32)


def kernel(
    runs, ways,
    q_hbm, k_hbm, v_hbm, rates_hbm, mix, sums_ref,
    rates, q_buf, k_buf, v_buf, acc, entering,
    s_loc, s_oth, c_tot, c_oth, p_in, p_out, e_mine, e_send, e_oth, ss_loc, ss_in,
    r_sem, q_sem, k_sem, v_sem, s_ss, s_rs, c_ss, c_rs, p_ss, p_rs, e_ss, e_rs, n_ss, n_rs,
):
    heads, length = q_buf.shape[0], q_buf.shape[1]
    half = heads // 2
    blocks = length // BLOCK
    groups = runs // GROUP
    me = lax.axis_index("seq")
    way = lax.axis_index("head")
    core = lax.rem(me, 2)
    x = lax.rem(me // 2, 2)
    z = me // GROUP
    core_peer = me + 1 - 2 * core
    x_peer = me + 2 - 4 * x
    own0 = core * half
    oth0 = (1 - core) * half
    core_f = core.astype(F32)
    x_f = x.astype(F32)

    def load(hbm, buf, sem, h):
        return pltpu.make_async_copy(hbm.at[:, pl.ds(pl.multiple_of(h * E, E), E)], buf.at[h], sem.at[h])

    def remote(src, dst, ss, rs, seq, head):
        return pltpu.make_async_remote_copy(
            src_ref=src, dst_ref=dst, send_sem=ss, recv_sem=rs,
            device_id={"seq": seq, "head": head}, device_id_type=pl.DeviceIdType.MESH,
        )

    def state_copy(k):
        return remote(s_loc.at[oth0 + k], s_oth.at[k], s_ss.at[k], s_rs.at[k], core_peer, way)

    def chip_copy(k):
        return remote(c_tot.at[k], c_oth.at[k], c_ss.at[k], c_rs.at[k], x_peer, way)

    def chain_copy(k):
        up = lax.rem(me + GROUP, runs)
        return remote(p_out.at[k], p_in.at[k], p_ss.at[k], p_rs.at[k], up, way)

    def carry_copy(k):
        return remote(e_send.at[k], e_oth.at[k], e_ss.at[k], e_rs.at[k], core_peer, way)

    def norm_copy(d):
        return remote(ss_loc, ss_in.at[d - 1], n_ss.at[d - 1], n_rs.at[d - 1], me, lax.rem(way + d, ways))

    def start_states(k, c):
        for h in (own0 + k, oth0 + k):
            load(k_hbm, k_buf, k_sem, h).start()
            load(v_hbm, v_buf, v_sem, h).start()
        return c

    def start_queries(k, c):
        for h in (own0 + k, oth0 + k):
            load(q_hbm, q_buf, q_sem, h).start()
        return c

    rates_copy = pltpu.make_async_copy(rates_hbm, rates, r_sem)
    rates_copy.start()
    lax.fori_loop(0, half, start_states, 0)
    lax.fori_loop(0, half, start_queries, 0)

    barrier = pltpu.get_barrier_semaphore()

    def greet(seq, head):
        pl.semaphore_signal(
            barrier, inc=1, device_id={"seq": seq, "head": head}, device_id_type=pl.DeviceIdType.MESH
        )

    greet(core_peer, way)
    greet(x_peer, way)
    for d in range(1, ways):
        greet(me, lax.rem(way + d, ways))

    @pl.when(z > 0)
    def _():
        greet(me - GROUP, way)

    @pl.when(z < groups - 1)
    def _():
        greet(me + GROUP, way)

    @pl.when(z == 0)
    def _():
        p_in[...] = jnp.zeros_like(p_in)

    acc[...] = jnp.zeros_like(acc)
    rates_copy.wait()

    def power(rate, steps):
        return jnp.exp(jnp.full((1, E), -rate * steps, F32))

    row = lax.broadcasted_iota(jnp.int32, (8, E), 0).astype(F32)

    def rising(rate):
        column = jnp.exp(-rate * (row + 1.0))
        while column.shape[0] < BLOCK:
            column = jnp.concatenate([column, column * power(rate, float(column.shape[0]))], axis=0)
        return column

    def falling(rate):
        column = jnp.exp(-rate * (7.0 - row))
        while column.shape[0] < BLOCK:
            column = jnp.concatenate([column * power(rate, float(column.shape[0])), column], axis=0)
        return column


    def local_states(k):
        pair = (oth0 + k, own0 + k)
        for h in pair:
            load(k_hbm, k_buf, k_sem, h).wait()
            load(v_hbm, v_buf, v_sem, h).wait()
        whole = [power(rates[h], float(BLOCK)) for h in pair]
        scale = [falling(rates[h]) for h in pair]
        state = [None, None]
        for b in range(blocks):
            rows = pl.ds(b * BLOCK, BLOCK)
            for n, h in enumerate(pair):
                scaled = (k_buf[h, rows, :].astype(F32) * scale[n]).astype(BF16)
                part = dot(scaled, v_buf[h, rows, :], (0, 0))
                state[n] = part if b == 0 else state[n] * whole[n] + part
                if b < blocks - 1:
                    entering[h, b] = state[n]
                else:
                    s_loc[h] = state[n]

    def chip_total(k):
        rate = rates[own0 + k]
        state_copy(k).wait_recv()
        mine = power(rate, length * (1.0 - core_f))
        other = power(rate, length * core_f)
        for p in range(CUTS):
            rows = pl.ds(p * PIECE, PIECE)
            c_tot[k * CUTS + p] = mine * s_loc[own0 + k, rows, :] + other * s_oth[k, rows, :]
            chip_copy(k * CUTS + p).start()

    def state_step(k, c):
        local_states(k)
        state_copy(k).start()
        chip_total(k - 1)
        return c

    local_states(0)
    pl.semaphore_wait(barrier, 2 + (ways - 1) + jnp.minimum(z, 1) + jnp.minimum(groups - 1 - z, 1))
    state_copy(0).start()
    lax.fori_loop(1, half, state_step, 0)
    chip_total(half - 1)

    small = E
    down = lax.broadcasted_iota(jnp.int32, (small, small), 0) - lax.broadcasted_iota(jnp.int32, (small, small), 1)
    down_f = down.astype(F32)
    left = (small - 1) - lax.broadcasted_iota(jnp.int32, (1, small), 1).astype(F32)
    blank = jnp.zeros((small, small), BF16)

    def attend(k):
        pair = (own0 + k, oth0 + k)
        for h in pair:
            load(q_hbm, q_buf, q_sem, h).wait()
        near = [jnp.where(down >= 0, jnp.exp(-rates[h] * jnp.maximum(down_f, 0.0)), 0.0) for h in pair]
        far = [rising(rates[h])[:small] * jnp.exp(-rates[h] * left) for h in pair]
        units = [(n, b) for n in range(2) for b in range(blocks)]

        def score(unit):
            rows = pl.ds(unit[1] * BLOCK, BLOCK)
            return dot(q_buf[pair[unit[0]], rows, :], k_buf[pair[unit[0]], rows, :], (1, 1))

        ahead = score(units[0])
        for at, (n, b) in enumerate(units):
            scores = ahead
            if at + 1 < len(units):
                ahead = score(units[at + 1])
            vals = v_buf[pair[n], pl.ds(b * BLOCK, BLOCK), :]
            top = jnp.concatenate([(scores[:small, :small] * near[n]).astype(BF16), blank], axis=1)
            low = jnp.concatenate(
                [(scores[small:, :small] * far[n]).astype(BF16), (scores[small:, small:] * near[n]).astype(BF16)],
                axis=1,
            )
            mix[pair[n], pl.ds(b * BLOCK, BLOCK), :] = dot(jnp.concatenate([top, low], axis=0), vals, (1, 0))

    def chain(s):
        k = s // CUTS
        rows = pl.ds(pl.multiple_of(lax.rem(s, CUTS) * PIECE, PIECE), PIECE)
        rate = rates[own0 + k]
        chip_copy(s).wait_recv()

        @pl.when(z > 0)
        def _():
            chain_copy(s).wait_recv()

        before = p_in[s]
        other = c_oth[s]
        two = 2.0 * length

        @pl.when(z < groups - 1)
        def _():
            total = power(rate, two * (1.0 - x_f)) * c_tot[s] + power(rate, two * x_f) * other
            p_out[s] = power(rate, 2.0 * two) * before + total
            chain_copy(s).start()

        chip = power(rate, two * x_f) * before + x_f * other

        @pl.when(core == 0)
        def _():
            e_mine[s] = chip
            e_send[s] = power(rate, float(length)) * chip + s_loc[own0 + k, rows, :]

        @pl.when(core == 1)
        def _():
            e_mine[s] = power(rate, float(length)) * chip + s_oth[k, rows, :]
            e_send[s] = chip

        carry_copy(s).start()

    def finish(k):
        pair = (own0 + k, oth0 + k)
        for p in range(CUTS):
            carry_copy(k * CUTS + p).wait_recv()
        parts = pl.ds(k * CUTS, CUTS)
        carry = (e_mine[parts].reshape(E, E), e_oth[parts].reshape(E, E))
        scale = [rising(rates[h]) for h in pair]
        for b in range(blocks):
            rows = pl.ds(b * BLOCK, BLOCK)
            squares = acc[rows, :]
            for n, h in enumerate(pair):
                state = carry[n]
                if b > 0:
                    state = power(rates[h], float(b * BLOCK)) * state + entering[h, b - 1]
                mixed = mix[h, rows, :] + scale[n] * dot(q_buf[h, rows, :], state.astype(BF16), (1, 0))
                mix[h, rows, :] = mixed
                squares = squares + mixed * mixed
            acc[rows, :] = squares

    top_lag = min(5 * (groups - 1) // 2, half)
    lag = jnp.minimum(5 * z // 2, half)

    def step(i, c):
        @pl.when(i < half)
        def _():
            attend(i)

        def turn(n, c):
            k = 2 * (i - lag) + n
            here = jnp.logical_and(k >= 0, k < half)

            @pl.when(here)
            def _():
                chain(k * CUTS)

            j = 2 * (i - top_lag) + n - 1

            @pl.when(jnp.logical_and(j >= 0, j < half))
            def _():
                finish(j)

            @pl.when(here)
            def _():
                for p in range(1, CUTS):
                    chain(k * CUTS + p)

            return c

        return lax.fori_loop(0, 2, turn, c)

    lax.fori_loop(0, max(half, top_lag + (half + 1) // 2 + 1), step, 0)

    slabs = length // E
    for g in range(slabs):
        ss_loc[pl.ds(g, 1), :] = jnp.sum(acc[pl.ds(g * E, E), :].T, axis=0, keepdims=True)
    for d in range(1, ways):
        norm_copy(d).start()
    for d in range(1, ways):
        norm_copy(d).wait_recv()
    sums = ss_loc[...]
    for d in range(1, ways):
        sums = sums + ss_in[d - 1]
    sums_ref[...] = sums

    def drain(k, c):
        state_copy(k).wait_send()
        for p in range(CUTS):
            chip_copy(k * CUTS + p).wait_send()
            carry_copy(k * CUTS + p).wait_send()

        @pl.when(z < groups - 1)
        def _():
            for p in range(CUTS):
                chain_copy(k * CUTS + p).wait_send()

        return c

    lax.fori_loop(0, half, drain, 0)
    for d in range(1, ways):
        norm_copy(d).wait_send()


def normalise(width, mixed_ref, sums_ref, gain_hbm, out_hbm, gain, ready, gain_sem, out_sem):
    slabs = mixed_ref.shape[1] // E
    fetch = pltpu.make_async_copy(gain_hbm, gain, gain_sem)
    fetch.start()

    def put(t):
        rows = pl.ds(pl.multiple_of(t * E, E), E)
        return pltpu.make_async_copy(ready.at[rows], out_hbm.at[rows], out_sem.at[t])

    fetch.wait()

    def slab(t, c):
        inverse = jnp.broadcast_to(lax.rsqrt(sums_ref[pl.ds(t, 1), :] / width + EPSILON), (E, E)).T
        rows = pl.ds(pl.multiple_of(t * E, E), E)
        for h in range(mixed_ref.shape[0]):
            cols = pl.ds(h * E, E)
            ready[rows, cols] = (mixed_ref[h, rows, :] * inverse * gain[:, cols]).astype(BF16)
        put(t).start()
        return c

    lax.fori_loop(0, slabs, slab, 0)

    def drain(t, c):
        put(t).wait()
        return c

    lax.fori_loop(0, slabs, drain, 0)


def body(runs, ways, queries, key_rows, value_rows, decay_rates, out_gain):
    length, columns = queries.shape
    heads = decay_rates.shape[0]
    half = heads // 2
    blocks = length // BLOCK
    dma = pltpu.SemaphoreType.DMA
    states = [pltpu.VMEM((half, E, E), F32)]
    sems = [dma((half,))]
    fixed = [pltpu.with_memory_space_constraint(a, pltpu.HBM) for a in (queries, key_rows, value_rows, decay_rates)]
    gain = pltpu.with_memory_space_constraint(out_gain.reshape(1, columns), pltpu.HBM)
    sums_shape = (length // E, E)
    mixed, sums = pl.pallas_call(
        functools.partial(kernel, runs, ways),
        out_shape=(jax.ShapeDtypeStruct((heads, length, E), F32), jax.ShapeDtypeStruct(sums_shape, F32)),
        in_specs=[pl.BlockSpec(memory_space=pltpu.HBM)] * 4,
        out_specs=(pl.BlockSpec(memory_space=pltpu.VMEM),) * 2,
        scratch_shapes=[pltpu.SMEM((heads,), F32)]
        + [pltpu.VMEM((heads, length, E), BF16)] * 3
        + [
            pltpu.VMEM((length, E), F32),
            pltpu.VMEM((heads, blocks - 1, E, E), F32),
            pltpu.VMEM((heads, E, E), F32),
        ]
        + states
        + [pltpu.VMEM((half * CUTS, PIECE, E), F32)] * 7
        + [pltpu.VMEM(sums_shape, F32), pltpu.VMEM((max(ways - 1, 1),) + sums_shape, F32)]
        + [dma]
        + [dma((heads,))] * 3
        + sems * 2
        + [dma((half * CUTS,))] * 6
        + [dma((max(ways - 1, 1),))] * 2,
        compiler_params=pltpu.CompilerParams(
            collective_id=0, has_side_effects=True, vmem_limit_bytes=40 * 1024 * 1024
        ),
        cost_estimate=pl.CostEstimate(
            flops=12 * length * BLOCK * heads * E, bytes_accessed=8 * length * heads * E, transcendentals=0
        ),
    )(*fixed)
    return pl.pallas_call(
        functools.partial(normalise, float(heads * ways * E)),
        out_shape=jax.ShapeDtypeStruct(queries.shape, BF16),
        in_specs=[pl.BlockSpec(memory_space=pltpu.VMEM)] * 2 + [pl.BlockSpec(memory_space=pltpu.HBM)],
        out_specs=pl.BlockSpec(memory_space=pltpu.HBM),
        scratch_shapes=[
            pltpu.VMEM((1, columns), F32),
            pltpu.VMEM(queries.shape, BF16),
            dma,
            dma((length // E,)),
        ],
        compiler_params=pltpu.CompilerParams(vmem_limit_bytes=16 * 1024 * 1024),
        cost_estimate=pl.CostEstimate(
            flops=3 * length * columns, bytes_accessed=4 * length * columns, transcendentals=0
        ),
    )(mixed, sums, gain)


def solution(mesh):
    placed = (P("seq", "head"), P("seq", "head"), P("seq", "head"), P("head"), P("head"))
    return jax.shard_map(
        functools.partial(body, mesh.shape["seq"], mesh.shape["head"]),
        mesh=mesh, in_specs=placed, out_specs=P("seq", "head"), check_vma=False,
    )
```

```python
import functools

import jax
import jax.numpy as jnp
from jax import lax
from jax.experimental import pallas as pl
from jax.experimental.pallas import tpu as pltpu
from jax.sharding import PartitionSpec as P

E = 128
BLOCK = 256
EPSILON = 1e-06
GROUP = 4
CUTS = 1
PIECE = E // CUTS
F32 = jnp.float32
BF16 = jnp.bfloat16


def dot(a, b, contract):
    return lax.dot_general(a, b, ((contract[:1], contract[1:]), ((), ())), preferred_element_type=F32)


def kernel(
    runs, ways,
    q_hbm, k_hbm, v_hbm, rates_hbm, mix, sums_ref,
    rates, q_buf, k_buf, v_buf, local, acc, entering,
    s_loc, s_oth, c_tot, c_oth, p_in, p_out, e_mine, e_send, e_oth, ss_loc, ss_in,
    r_sem, q_sem, k_sem, v_sem, s_ss, s_rs, c_ss, c_rs, p_ss, p_rs, e_ss, e_rs, n_ss, n_rs,
):
    heads, length = q_buf.shape[0], q_buf.shape[1]
    half = heads // 2
    blocks = length // BLOCK
    groups = runs // GROUP
    me = lax.axis_index("seq")
    way = lax.axis_index("head")
    core = lax.rem(me, 2)
    x = lax.rem(me // 2, 2)
    z = me // GROUP
    core_peer = me + 1 - 2 * core
    x_peer = me + 2 - 4 * x
    own0 = core * half
    oth0 = (1 - core) * half
    core_f = core.astype(F32)
    x_f = x.astype(F32)

    def load(hbm, buf, sem, h):
        return pltpu.make_async_copy(hbm.at[:, pl.ds(pl.multiple_of(h * E, E), E)], buf.at[h], sem.at[h])

    def remote(src, dst, ss, rs, seq, head):
        return pltpu.make_async_remote_copy(
            src_ref=src, dst_ref=dst, send_sem=ss, recv_sem=rs,
            device_id={"seq": seq, "head": head}, device_id_type=pl.DeviceIdType.MESH,
        )

    def state_copy(k):
        return remote(s_loc.at[oth0 + k], s_oth.at[k], s_ss.at[k], s_rs.at[k], core_peer, way)

    def chip_copy(k):
        return remote(c_tot.at[k], c_oth.at[k], c_ss.at[k], c_rs.at[k], x_peer, way)

    def chain_copy(k):
        up = lax.rem(me + GROUP, runs)
        return remote(p_out.at[k], p_in.at[k], p_ss.at[k], p_rs.at[k], up, way)

    def carry_copy(k):
        return remote(e_send.at[k], e_oth.at[k], e_ss.at[k], e_rs.at[k], core_peer, way)

    def norm_copy(d):
        return remote(ss_loc, ss_in.at[d - 1], n_ss.at[d - 1], n_rs.at[d - 1], me, lax.rem(way + d, ways))

    def start_states(k, c):
        for h in (own0 + k, oth0 + k):
            load(k_hbm, k_buf, k_sem, h).start()
            load(v_hbm, v_buf, v_sem, h).start()
        return c

    def start_queries(k, c):
        for h in (own0 + k, oth0 + k):
            load(q_hbm, q_buf, q_sem, h).start()
        return c

    rates_copy = pltpu.make_async_copy(rates_hbm, rates, r_sem)
    rates_copy.start()
    lax.fori_loop(0, half, start_states, 0)
    lax.fori_loop(0, half, start_queries, 0)

    barrier = pltpu.get_barrier_semaphore()

    def greet(seq, head):
        pl.semaphore_signal(
            barrier, inc=1, device_id={"seq": seq, "head": head}, device_id_type=pl.DeviceIdType.MESH
        )

    greet(core_peer, way)
    greet(x_peer, way)
    for d in range(1, ways):
        greet(me, lax.rem(way + d, ways))

    @pl.when(z > 0)
    def _():
        greet(me - GROUP, way)

    @pl.when(z < groups - 1)
    def _():
        greet(me + GROUP, way)

    @pl.when(z == 0)
    def _():
        p_in[...] = jnp.zeros_like(p_in)

    acc[...] = jnp.zeros_like(acc)
    rates_copy.wait()

    def power(rate, steps):
        return jnp.exp(jnp.full((1, E), -rate * steps, F32))

    row = lax.broadcasted_iota(jnp.int32, (8, E), 0).astype(F32)

    def rising(rate):
        column = jnp.exp(-rate * (row + 1.0))
        while column.shape[0] < BLOCK:
            column = jnp.concatenate([column, column * power(rate, float(column.shape[0]))], axis=0)
        return column

    def falling(rate):
        column = jnp.exp(-rate * (7.0 - row))
        while column.shape[0] < BLOCK:
            column = jnp.concatenate([column * power(rate, float(column.shape[0])), column], axis=0)
        return column


    def local_states(k):
        pair = (oth0 + k, own0 + k)
        for h in pair:
            load(k_hbm, k_buf, k_sem, h).wait()
            load(v_hbm, v_buf, v_sem, h).wait()
        whole = [power(rates[h], float(BLOCK)) for h in pair]
        scale = [falling(rates[h]) for h in pair]
        state = [None, None]
        for b in range(blocks):
            rows = pl.ds(b * BLOCK, BLOCK)
            for n, h in enumerate(pair):
                scaled = (k_buf[h, rows, :].astype(F32) * scale[n]).astype(BF16)
                part = dot(scaled, v_buf[h, rows, :], (0, 0))
                state[n] = part if b == 0 else state[n] * whole[n] + part
                if b < blocks - 1:
                    entering[h, b] = state[n]
                else:
                    s_loc[h] = state[n]

    def chip_total(k):
        rate = rates[own0 + k]
        state_copy(k).wait_recv()
        mine = power(rate, length * (1.0 - core_f))
        other = power(rate, length * core_f)
        for p in range(CUTS):
            rows = pl.ds(p * PIECE, PIECE)
            c_tot[k * CUTS + p] = mine * s_loc[own0 + k, rows, :] + other * s_oth[k, rows, :]
            chip_copy(k * CUTS + p).start()

    def state_step(k, c):
        local_states(k)
        state_copy(k).start()
        chip_total(k - 1)
        return c

    local_states(0)
    pl.semaphore_wait(barrier, 2 + (ways - 1) + jnp.minimum(z, 1) + jnp.minimum(groups - 1 - z, 1))
    state_copy(0).start()
    lax.fori_loop(1, half, state_step, 0)
    chip_total(half - 1)

    small = E
    down = lax.broadcasted_iota(jnp.int32, (small, small), 0) - lax.broadcasted_iota(jnp.int32, (small, small), 1)
    down_f = down.astype(F32)
    left = (small - 1) - lax.broadcasted_iota(jnp.int32, (1, small), 1).astype(F32)
    blank = jnp.zeros((small, small), BF16)

    def attend(k):
        pair = (own0 + k, oth0 + k)
        for h in pair:
            load(q_hbm, q_buf, q_sem, h).wait()
        near = [jnp.where(down >= 0, jnp.exp(-rates[h] * jnp.maximum(down_f, 0.0)), 0.0) for h in pair]
        far = [rising(rates[h])[:small] * jnp.exp(-rates[h] * left) for h in pair]
        units = [(n, b) for n in range(2) for b in range(blocks)]

        def score(unit):
            rows = pl.ds(unit[1] * BLOCK, BLOCK)
            return dot(q_buf[pair[unit[0]], rows, :], k_buf[pair[unit[0]], rows, :], (1, 1))

        ahead = score(units[0])
        for at, (n, b) in enumerate(units):
            scores = ahead
            if at + 1 < len(units):
                ahead = score(units[at + 1])
            vals = v_buf[pair[n], pl.ds(b * BLOCK, BLOCK), :]
            top = jnp.concatenate([(scores[:small, :small] * near[n]).astype(BF16), blank], axis=1)
            low = jnp.concatenate(
                [(scores[small:, :small] * far[n]).astype(BF16), (scores[small:, small:] * near[n]).astype(BF16)],
                axis=1,
            )
            local[pair[n], pl.ds(b * BLOCK, BLOCK), :] = dot(jnp.concatenate([top, low], axis=0), vals, (1, 0))

    def chain(s):
        k = s // CUTS
        rows = pl.ds(pl.multiple_of(lax.rem(s, CUTS) * PIECE, PIECE), PIECE)
        rate = rates[own0 + k]
        chip_copy(s).wait_recv()

        @pl.when(z > 0)
        def _():
            chain_copy(s).wait_recv()

        before = p_in[s]
        other = c_oth[s]
        two = 2.0 * length

        @pl.when(z < groups - 1)
        def _():
            total = power(rate, two * (1.0 - x_f)) * c_tot[s] + power(rate, two * x_f) * other
            p_out[s] = power(rate, 2.0 * two) * before + total
            chain_copy(s).start()

        chip = power(rate, two * x_f) * before + x_f * other

        @pl.when(core == 0)
        def _():
            e_mine[s] = chip
            e_send[s] = power(rate, float(length)) * chip + s_loc[own0 + k, rows, :]

        @pl.when(core == 1)
        def _():
            e_mine[s] = power(rate, float(length)) * chip + s_oth[k, rows, :]
            e_send[s] = chip

        carry_copy(s).start()

    def finish(k):
        pair = (own0 + k, oth0 + k)
        for p in range(CUTS):
            carry_copy(k * CUTS + p).wait_recv()
        parts = pl.ds(k * CUTS, CUTS)
        carry = (e_mine[parts].reshape(E, E), e_oth[parts].reshape(E, E))
        scale = [rising(rates[h]) for h in pair]
        units = [(n, b) for b in range(blocks) for n in range(2)]

        def carried(unit):
            n, b = unit
            h = pair[n]
            state = carry[n]
            if b > 0:
                state = power(rates[h], float(b * BLOCK)) * state + entering[h, b - 1]
            return dot(q_buf[h, pl.ds(b * BLOCK, BLOCK), :], state.astype(BF16), (1, 0))

        ahead = carried(units[0])
        squares = None
        for at, (n, b) in enumerate(units):
            now = ahead
            if at + 1 < len(units):
                ahead = carried(units[at + 1])
            rows = pl.ds(b * BLOCK, BLOCK)
            mixed = local[pair[n], rows, :] + scale[n] * now
            mix[pair[n], rows, :] = mixed
            squares = mixed * mixed if n == 0 else squares + mixed * mixed
            if n == 1:
                acc[rows, :] += squares

    top_lag = half - 1
    lag = jnp.where(z == groups - 1, top_lag, jnp.minimum(z, top_lag))

    def step(i, c):
        @pl.when(i < half)
        def _():
            attend(i)

        def turn(n, c):
            k = 2 * (i - lag) + n
            here = jnp.logical_and(k >= 0, k < half)

            @pl.when(here)
            def _():
                chain(k * CUTS)

            j = 2 * (i - top_lag) + n - 1

            @pl.when(jnp.logical_and(j >= 0, j < half))
            def _():
                finish(j)

            @pl.when(here)
            def _():
                for p in range(1, CUTS):
                    chain(k * CUTS + p)

            return c

        return lax.fori_loop(0, 2, turn, c)

    lax.fori_loop(0, max(half, top_lag + (half + 1) // 2 + 1), step, 0)

    slabs = length // E
    for g in range(slabs):
        ss_loc[pl.ds(g, 1), :] = jnp.sum(acc[pl.ds(g * E, E), :].T, axis=0, keepdims=True)
    for d in range(1, ways):
        norm_copy(d).start()
    for d in range(1, ways):
        norm_copy(d).wait_recv()
    sums = ss_loc[...]
    for d in range(1, ways):
        sums = sums + ss_in[d - 1]
    sums_ref[...] = sums

    def drain(k, c):
        state_copy(k).wait_send()
        for p in range(CUTS):
            chip_copy(k * CUTS + p).wait_send()
            carry_copy(k * CUTS + p).wait_send()

        @pl.when(z < groups - 1)
        def _():
            for p in range(CUTS):
                chain_copy(k * CUTS + p).wait_send()

        return c

    lax.fori_loop(0, half, drain, 0)
    for d in range(1, ways):
        norm_copy(d).wait_send()


def normalise(width, mixed_ref, sums_ref, gain_hbm, out_hbm, gain, ready, gain_sem, out_sem):
    slabs = mixed_ref.shape[1] // E
    fetch = pltpu.make_async_copy(gain_hbm, gain, gain_sem)
    fetch.start()

    def put(t):
        rows = pl.ds(pl.multiple_of(t * E, E), E)
        return pltpu.make_async_copy(ready.at[rows], out_hbm.at[rows], out_sem.at[t])

    fetch.wait()

    def slab(t, c):
        inverse = jnp.broadcast_to(lax.rsqrt(sums_ref[pl.ds(t, 1), :] / width + EPSILON), (E, E)).T
        rows = pl.ds(pl.multiple_of(t * E, E), E)
        for h in range(mixed_ref.shape[0]):
            cols = pl.ds(h * E, E)
            ready[rows, cols] = (mixed_ref[h, rows, :] * inverse * gain[:, cols]).astype(BF16)
        put(t).start()
        return c

    lax.fori_loop(0, slabs, slab, 0)

    def drain(t, c):
        put(t).wait()
        return c

    lax.fori_loop(0, slabs, drain, 0)


def body(runs, ways, queries, key_rows, value_rows, decay_rates, out_gain):
    length, columns = queries.shape
    heads = decay_rates.shape[0]
    half = heads // 2
    blocks = length // BLOCK
    dma = pltpu.SemaphoreType.DMA
    states = [pltpu.VMEM((half, E, E), F32)]
    sems = [dma((half,))]
    fixed = [pltpu.with_memory_space_constraint(a, pltpu.HBM) for a in (queries, key_rows, value_rows, decay_rates)]
    gain = pltpu.with_memory_space_constraint(out_gain.reshape(1, columns), pltpu.HBM)
    sums_shape = (length // E, E)
    mixed, sums = pl.pallas_call(
        functools.partial(kernel, runs, ways),
        out_shape=(jax.ShapeDtypeStruct((heads, length, E), F32), jax.ShapeDtypeStruct(sums_shape, F32)),
        in_specs=[pl.BlockSpec(memory_space=pltpu.HBM)] * 4,
        out_specs=(pl.BlockSpec(memory_space=pltpu.VMEM),) * 2,
        scratch_shapes=[pltpu.SMEM((heads,), F32)]
        + [pltpu.VMEM((heads, length, E), BF16)] * 3
        + [
            pltpu.VMEM((heads, length, E), F32),
            pltpu.VMEM((length, E), F32),
            pltpu.VMEM((heads, blocks - 1, E, E), F32),
            pltpu.VMEM((heads, E, E), F32),
        ]
        + states
        + [pltpu.VMEM((half * CUTS, PIECE, E), F32)] * 7
        + [pltpu.VMEM(sums_shape, F32), pltpu.VMEM((max(ways - 1, 1),) + sums_shape, F32)]
        + [dma]
        + [dma((heads,))] * 3
        + sems * 2
        + [dma((half * CUTS,))] * 6
        + [dma((max(ways - 1, 1),))] * 2,
        compiler_params=pltpu.CompilerParams(
            collective_id=0, has_side_effects=True, vmem_limit_bytes=40 * 1024 * 1024
        ),
        cost_estimate=pl.CostEstimate(
            flops=12 * length * BLOCK * heads * E, bytes_accessed=8 * length * heads * E, transcendentals=0
        ),
    )(*fixed)
    return pl.pallas_call(
        functools.partial(normalise, float(heads * ways * E)),
        out_shape=jax.ShapeDtypeStruct(queries.shape, BF16),
        in_specs=[pl.BlockSpec(memory_space=pltpu.VMEM)] * 2 + [pl.BlockSpec(memory_space=pltpu.HBM)],
        out_specs=pl.BlockSpec(memory_space=pltpu.HBM),
        scratch_shapes=[
            pltpu.VMEM((1, columns), F32),
            pltpu.VMEM(queries.shape, BF16),
            dma,
            dma((length // E,)),
        ],
        compiler_params=pltpu.CompilerParams(vmem_limit_bytes=16 * 1024 * 1024),
        cost_estimate=pl.CostEstimate(
            flops=3 * length * columns, bytes_accessed=4 * length * columns, transcendentals=0
        ),
    )(mixed, sums, gain)


def solution(mesh):
    placed = (P("seq", "head"), P("seq", "head"), P("seq", "head"), P("head"), P("head"))
    return jax.shard_map(
        functools.partial(body, mesh.shape["seq"], mesh.shape["head"]),
        mesh=mesh, in_specs=placed, out_specs=P("seq", "head"), check_vma=False,
    )
```

```python
import functools

import jax
import jax.numpy as jnp
from jax import lax
from jax.experimental import pallas as pl
from jax.experimental.pallas import tpu as pltpu
from jax.sharding import PartitionSpec as P

E = 128
BLOCK = 256
EPSILON = 1e-06
GROUP = 4
F32 = jnp.float32
BF16 = jnp.bfloat16


def dot(a, b, contract):
    return lax.dot_general(a, b, ((contract[:1], contract[1:]), ((), ())), preferred_element_type=F32)


def kernel(
    runs, ways,
    q_hbm, k_hbm, v_hbm, rates_hbm, mix, sums_ref,
    rates, q_buf, k_buf, v_buf, local, acc, entering,
    s_loc, s_oth, c_tot, c_oth, p_in, p_out, g_out, g_in, e_mine, e_send, e_oth, ss_loc, ss_in,
    r_sem, q_sem, k_sem, v_sem, s_ss, s_rs, c_ss, c_rs, p_ss, p_rs, g_ss, g_rs, e_ss, e_rs, n_ss, n_rs,
):
    heads, length = q_buf.shape[0], q_buf.shape[1]
    half = heads // 2
    quarter = half // 2
    blocks = length // BLOCK
    groups = runs // GROUP
    me = lax.axis_index("seq")
    way = lax.axis_index("head")
    core = lax.rem(me, 2)
    x = lax.rem(me // 2, 2)
    z = me // GROUP
    core_peer = me + 1 - 2 * core
    x_peer = me + 2 - 4 * x
    own0 = core * half
    oth0 = (1 - core) * half
    core_f = core.astype(F32)
    x_f = x.astype(F32)

    def load(hbm, buf, sem, h):
        return pltpu.make_async_copy(hbm.at[:, pl.ds(pl.multiple_of(h * E, E), E)], buf.at[h], sem.at[h])

    def remote(src, dst, ss, rs, seq, head):
        return pltpu.make_async_remote_copy(
            src_ref=src, dst_ref=dst, send_sem=ss, recv_sem=rs,
            device_id={"seq": seq, "head": head}, device_id_type=pl.DeviceIdType.MESH,
        )

    def state_copy(k):
        return remote(s_loc.at[oth0 + k], s_oth.at[k], s_ss.at[k], s_rs.at[k], core_peer, way)

    def chip_copy(m):
        return remote(c_tot.at[2 * m + 1 - x], c_oth.at[m], c_ss.at[m], c_rs.at[m], x_peer, way)

    def chain_copy(m):
        up = lax.rem(me + GROUP, runs)
        return remote(p_out.at[m], p_in.at[m], p_ss.at[m], p_rs.at[m], up, way)

    def return_copy(m):
        return remote(g_out.at[m], g_in.at[m], g_ss.at[m], g_rs.at[m], x_peer, way)

    def carry_copy(k):
        return remote(e_send.at[k], e_oth.at[k], e_ss.at[k], e_rs.at[k], core_peer, way)

    def norm_copy(d):
        return remote(ss_loc, ss_in.at[d - 1], n_ss.at[d - 1], n_rs.at[d - 1], me, lax.rem(way + d, ways))

    def start_states(k, c):
        for h in (own0 + k, oth0 + k):
            load(k_hbm, k_buf, k_sem, h).start()
            load(v_hbm, v_buf, v_sem, h).start()
        return c

    def start_queries(k, c):
        for h in (own0 + k, oth0 + k):
            load(q_hbm, q_buf, q_sem, h).start()
        return c

    rates_copy = pltpu.make_async_copy(rates_hbm, rates, r_sem)
    rates_copy.start()
    lax.fori_loop(0, half, start_states, 0)
    lax.fori_loop(0, half, start_queries, 0)

    barrier = pltpu.get_barrier_semaphore()

    def greet(seq, head):
        pl.semaphore_signal(
            barrier, inc=1, device_id={"seq": seq, "head": head}, device_id_type=pl.DeviceIdType.MESH
        )

    greet(core_peer, way)
    greet(x_peer, way)
    for d in range(1, ways):
        greet(me, lax.rem(way + d, ways))

    @pl.when(z > 0)
    def _():
        greet(me - GROUP, way)

    @pl.when(z < groups - 1)
    def _():
        greet(me + GROUP, way)

    @pl.when(z == 0)
    def _():
        p_in[...] = jnp.zeros_like(p_in)

    acc[...] = jnp.zeros_like(acc)
    rates_copy.wait()

    def power(rate, steps):
        return jnp.exp(jnp.full((1, E), -rate * steps, F32))

    row = lax.broadcasted_iota(jnp.int32, (8, E), 0).astype(F32)

    def rising(rate):
        column = jnp.exp(-rate * (row + 1.0))
        while column.shape[0] < BLOCK:
            column = jnp.concatenate([column, column * power(rate, float(column.shape[0]))], axis=0)
        return column

    def falling(rate):
        column = jnp.exp(-rate * (7.0 - row))
        while column.shape[0] < BLOCK:
            column = jnp.concatenate([column * power(rate, float(column.shape[0])), column], axis=0)
        return column


    def local_states(k):
        pair = (oth0 + k, own0 + k)
        for h in pair:
            load(k_hbm, k_buf, k_sem, h).wait()
            load(v_hbm, v_buf, v_sem, h).wait()
        whole = [power(rates[h], float(BLOCK)) for h in pair]
        scale = [falling(rates[h]) for h in pair]
        state = [None, None]
        for b in range(blocks):
            rows = pl.ds(b * BLOCK, BLOCK)
            for n, h in enumerate(pair):
                scaled = (k_buf[h, rows, :].astype(F32) * scale[n]).astype(BF16)
                part = dot(scaled, v_buf[h, rows, :], (0, 0))
                state[n] = part if b == 0 else state[n] * whole[n] + part
                if b < blocks - 1:
                    entering[h, b] = state[n]
                else:
                    s_loc[h] = state[n]

    def chip_total(k):
        rate = rates[own0 + k]
        state_copy(k).wait_recv()
        mine = power(rate, length * (1.0 - core_f))
        other = power(rate, length * core_f)
        c_tot[k] = mine * s_loc[own0 + k] + other * s_oth[k]

        @pl.when(lax.rem(k, 2) != x)
        def _():
            chip_copy(k // 2).start()

    def state_step(k, c):
        local_states(k)
        state_copy(k).start()
        chip_total(k - 1)
        return c

    local_states(0)
    pl.semaphore_wait(barrier, 2 + (ways - 1) + jnp.minimum(z, 1) + jnp.minimum(groups - 1 - z, 1))
    state_copy(0).start()
    lax.fori_loop(1, half, state_step, 0)
    chip_total(half - 1)

    small = E
    down = lax.broadcasted_iota(jnp.int32, (small, small), 0) - lax.broadcasted_iota(jnp.int32, (small, small), 1)
    down_f = down.astype(F32)
    left = (small - 1) - lax.broadcasted_iota(jnp.int32, (1, small), 1).astype(F32)
    blank = jnp.zeros((small, small), BF16)

    def attend(k):
        pair = (own0 + k, oth0 + k)
        for h in pair:
            load(q_hbm, q_buf, q_sem, h).wait()
        near = [jnp.where(down >= 0, jnp.exp(-rates[h] * jnp.maximum(down_f, 0.0)), 0.0) for h in pair]
        far = [rising(rates[h])[:small] * jnp.exp(-rates[h] * left) for h in pair]
        units = [(n, b) for n in range(2) for b in range(blocks)]

        def score(unit):
            rows = pl.ds(unit[1] * BLOCK, BLOCK)
            return dot(q_buf[pair[unit[0]], rows, :], k_buf[pair[unit[0]], rows, :], (1, 1))

        ahead = score(units[0])
        for at, (n, b) in enumerate(units):
            scores = ahead
            if at + 1 < len(units):
                ahead = score(units[at + 1])
            vals = v_buf[pair[n], pl.ds(b * BLOCK, BLOCK), :]
            top = jnp.concatenate([(scores[:small, :small] * near[n]).astype(BF16), blank], axis=1)
            low = jnp.concatenate(
                [(scores[small:, :small] * far[n]).astype(BF16), (scores[small:, small:] * near[n]).astype(BF16)],
                axis=1,
            )
            local[pair[n], pl.ds(b * BLOCK, BLOCK), :] = dot(jnp.concatenate([top, low], axis=0), vals, (1, 0))

    def share(k, chip):
        length_on = power(rates[own0 + k], float(length))

        @pl.when(core == 0)
        def _():
            e_mine[k] = chip
            e_send[k] = length_on * chip + s_loc[own0 + k]

        @pl.when(core == 1)
        def _():
            e_mine[k] = length_on * chip + s_oth[k]
            e_send[k] = chip

        carry_copy(k).start()

    def chain(m):
        k = 2 * m + x
        rate = rates[own0 + k]
        chip_copy(m).wait_recv()

        @pl.when(z > 0)
        def _():
            chain_copy(m).wait_recv()

        before = p_in[m]
        mine = c_tot[k]
        other = c_oth[m]
        chip_on = power(rate, 2.0 * length)
        second = chip_on * before + ((1.0 - x_f) * mine + x_f * other)

        @pl.when(z < groups - 1)
        def _():
            p_out[m] = chip_on * second + (x_f * mine + (1.0 - x_f) * other)
            chain_copy(m).start()

        g_out[m] = x_f * before + (1.0 - x_f) * second
        return_copy(m).start()
        share(k, (1.0 - x_f) * before + x_f * second)

    def relay(m):
        return_copy(m).wait_recv()
        share(2 * m + 1 - x, g_in[m])

    def finish(k):
        pair = (own0 + k, oth0 + k)
        carry_copy(k).wait_recv()
        carry = (e_mine[k], e_oth[k])
        scale = [rising(rates[h]) for h in pair]
        units = [(n, b) for b in range(blocks) for n in range(2)]

        def carried(unit):
            n, b = unit
            h = pair[n]
            state = carry[n]
            if b > 0:
                state = power(rates[h], float(b * BLOCK)) * state + entering[h, b - 1]
            return dot(q_buf[h, pl.ds(b * BLOCK, BLOCK), :], state.astype(BF16), (1, 0))

        ahead = carried(units[0])
        squares = None
        for at, (n, b) in enumerate(units):
            now = ahead
            if at + 1 < len(units):
                ahead = carried(units[at + 1])
            rows = pl.ds(b * BLOCK, BLOCK)
            mixed = local[pair[n], rows, :] + scale[n] * now
            mix[pair[n], rows, :] = mixed
            squares = mixed * mixed if n == 0 else squares + mixed * mixed
            if n == 1:
                acc[rows, :] += squares

    top_lag = half - 1
    lag = jnp.where(z == groups - 1, top_lag, jnp.minimum(z, top_lag))

    def step(i, c):
        @pl.when(i < half)
        def _():
            attend(i)

        def turn(n, c):
            m = 2 * (i - lag) + n

            @pl.when(jnp.logical_and(m >= 0, m < quarter))
            def _():
                chain(m)

            r = 2 * (i - top_lag) + n - 1

            @pl.when(jnp.logical_and(r >= 0, r < quarter))
            def _():
                relay(r)
                finish(2 * r + x)
                finish(2 * r + 1 - x)

            return c

        return lax.fori_loop(0, 2, turn, c)

    lax.fori_loop(0, max(half, top_lag + (quarter + 1) // 2 + 1), step, 0)

    slabs = length // E
    for g in range(slabs):
        ss_loc[pl.ds(g, 1), :] = jnp.sum(acc[pl.ds(g * E, E), :].T, axis=0, keepdims=True)
    for d in range(1, ways):
        norm_copy(d).start()
    for d in range(1, ways):
        norm_copy(d).wait_recv()
    sums = ss_loc[...]
    for d in range(1, ways):
        sums = sums + ss_in[d - 1]
    sums_ref[...] = sums

    def drain(k, c):
        state_copy(k).wait_send()
        carry_copy(k).wait_send()
        return c

    def drain_links(m, c):
        chip_copy(m).wait_send()
        return_copy(m).wait_send()

        @pl.when(z < groups - 1)
        def _():
            chain_copy(m).wait_send()

        return c

    lax.fori_loop(0, quarter, drain_links, 0)
    lax.fori_loop(0, half, drain, 0)
    for d in range(1, ways):
        norm_copy(d).wait_send()


def normalise(width, mixed_ref, sums_ref, gain_hbm, out_hbm, gain, ready, gain_sem, out_sem):
    slabs = mixed_ref.shape[1] // E
    fetch = pltpu.make_async_copy(gain_hbm, gain, gain_sem)
    fetch.start()

    def put(t):
        rows = pl.ds(pl.multiple_of(t * E, E), E)
        return pltpu.make_async_copy(ready.at[rows], out_hbm.at[rows], out_sem.at[t])

    fetch.wait()

    def slab(t, c):
        inverse = jnp.broadcast_to(lax.rsqrt(sums_ref[pl.ds(t, 1), :] / width + EPSILON), (E, E)).T
        rows = pl.ds(pl.multiple_of(t * E, E), E)
        for h in range(mixed_ref.shape[0]):
            cols = pl.ds(h * E, E)
            ready[rows, cols] = (mixed_ref[h, rows, :] * inverse * gain[:, cols]).astype(BF16)
        put(t).start()
        return c

    lax.fori_loop(0, slabs, slab, 0)

    def drain(t, c):
        put(t).wait()
        return c

    lax.fori_loop(0, slabs, drain, 0)


def body(runs, ways, queries, key_rows, value_rows, decay_rates, out_gain):
    length, columns = queries.shape
    heads = decay_rates.shape[0]
    half = heads // 2
    quarter = half // 2
    blocks = length // BLOCK
    dma = pltpu.SemaphoreType.DMA
    states = [pltpu.VMEM((half, E, E), F32)]
    sems = [dma((half,))]
    fixed = [pltpu.with_memory_space_constraint(a, pltpu.HBM) for a in (queries, key_rows, value_rows, decay_rates)]
    gain = pltpu.with_memory_space_constraint(out_gain.reshape(1, columns), pltpu.HBM)
    sums_shape = (length // E, E)
    mixed, sums = pl.pallas_call(
        functools.partial(kernel, runs, ways),
        out_shape=(jax.ShapeDtypeStruct((heads, length, E), F32), jax.ShapeDtypeStruct(sums_shape, F32)),
        in_specs=[pl.BlockSpec(memory_space=pltpu.HBM)] * 4,
        out_specs=(pl.BlockSpec(memory_space=pltpu.VMEM),) * 2,
        scratch_shapes=[pltpu.SMEM((heads,), F32)]
        + [pltpu.VMEM((heads, length, E), BF16)] * 3
        + [
            pltpu.VMEM((heads, length, E), F32),
            pltpu.VMEM((length, E), F32),
            pltpu.VMEM((heads, blocks - 1, E, E), F32),
            pltpu.VMEM((heads, E, E), F32),
        ]
        + states
        + states
        + [pltpu.VMEM((quarter, E, E), F32)] * 5
        + states * 3
        + [pltpu.VMEM(sums_shape, F32), pltpu.VMEM((max(ways - 1, 1),) + sums_shape, F32)]
        + [dma]
        + [dma((heads,))] * 3
        + sems * 2
        + [dma((quarter,))] * 6
        + sems * 2
        + [dma((max(ways - 1, 1),))] * 2,
        compiler_params=pltpu.CompilerParams(
            collective_id=0, has_side_effects=True, vmem_limit_bytes=40 * 1024 * 1024
        ),
        cost_estimate=pl.CostEstimate(
            flops=12 * length * BLOCK * heads * E, bytes_accessed=8 * length * heads * E, transcendentals=0
        ),
    )(*fixed)
    return pl.pallas_call(
        functools.partial(normalise, float(heads * ways * E)),
        out_shape=jax.ShapeDtypeStruct(queries.shape, BF16),
        in_specs=[pl.BlockSpec(memory_space=pltpu.VMEM)] * 2 + [pl.BlockSpec(memory_space=pltpu.HBM)],
        out_specs=pl.BlockSpec(memory_space=pltpu.HBM),
        scratch_shapes=[
            pltpu.VMEM((1, columns), F32),
            pltpu.VMEM(queries.shape, BF16),
            dma,
            dma((length // E,)),
        ],
        compiler_params=pltpu.CompilerParams(vmem_limit_bytes=16 * 1024 * 1024),
        cost_estimate=pl.CostEstimate(
            flops=3 * length * columns, bytes_accessed=4 * length * columns, transcendentals=0
        ),
    )(mixed, sums, gain)


def solution(mesh):
    placed = (P("seq", "head"), P("seq", "head"), P("seq", "head"), P("head"), P("head"))
    return jax.shard_map(
        functools.partial(body, mesh.shape["seq"], mesh.shape["head"]),
        mesh=mesh, in_specs=placed, out_specs=P("seq", "head"), check_vma=False,
    )
```

```python
import functools

import jax
import jax.numpy as jnp
from jax import lax
from jax.experimental import pallas as pl
from jax.experimental.pallas import tpu as pltpu
from jax.sharding import PartitionSpec as P

E = 128
BLOCK = 256
EPSILON = 1e-06
GROUP = 4
F32 = jnp.float32
BF16 = jnp.bfloat16


def dot(a, b, contract):
    return lax.dot_general(a, b, ((contract[:1], contract[1:]), ((), ())), preferred_element_type=F32)


def kernel(
    runs, ways,
    q_hbm, k_hbm, v_hbm, rates_hbm, mix, sums_ref,
    rates, q_buf, k_buf, v_buf, local, acc, entering,
    s_loc, s_oth, c_tot, c_oth, p_in, p_out, g_out, g_in, e_mine, e_send, e_oth, ss_loc, ss_in,
    r_sem, q_sem, k_sem, v_sem, s_ss, s_rs, c_ss, c_rs, p_ss, p_rs, g_ss, g_rs, e_ss, e_rs, n_ss, n_rs,
):
    heads, length = q_buf.shape[0], q_buf.shape[1]
    half = heads // 2
    quarter = half // 2
    blocks = length // BLOCK
    groups = runs // GROUP
    me = lax.axis_index("seq")
    way = lax.axis_index("head")
    core = lax.rem(me, 2)
    x = lax.rem(me // 2, 2)
    z = me // GROUP
    core_peer = me + 1 - 2 * core
    x_peer = me + 2 - 4 * x
    own0 = core * half
    oth0 = (1 - core) * half
    core_f = core.astype(F32)
    x_f = x.astype(F32)

    def load(hbm, buf, sem, h):
        return pltpu.make_async_copy(hbm.at[:, pl.ds(pl.multiple_of(h * E, E), E)], buf.at[h], sem.at[h])

    def remote(src, dst, ss, rs, seq, head):
        return pltpu.make_async_remote_copy(
            src_ref=src, dst_ref=dst, send_sem=ss, recv_sem=rs,
            device_id={"seq": seq, "head": head}, device_id_type=pl.DeviceIdType.MESH,
        )

    def state_copy(k):
        return remote(s_loc.at[oth0 + k], s_oth.at[k], s_ss.at[k], s_rs.at[k], core_peer, way)

    def chip_copy(m):
        return remote(c_tot.at[2 * m + 1 - x], c_oth.at[m], c_ss.at[m], c_rs.at[m], x_peer, way)

    def chain_copy(m):
        up = lax.rem(me + GROUP, runs)
        return remote(p_out.at[m], p_in.at[m], p_ss.at[m], p_rs.at[m], up, way)

    def return_copy(m):
        return remote(g_out.at[m], g_in.at[m], g_ss.at[m], g_rs.at[m], x_peer, way)

    def carry_copy(k):
        return remote(e_send.at[k], e_oth.at[k], e_ss.at[k], e_rs.at[k], core_peer, way)

    def norm_copy(d):
        return remote(ss_loc, ss_in.at[d - 1], n_ss.at[d - 1], n_rs.at[d - 1], me, lax.rem(way + d, ways))

    def start_states(k, c):
        for h in (own0 + k, oth0 + k):
            load(k_hbm, k_buf, k_sem, h).start()
            load(v_hbm, v_buf, v_sem, h).start()
        return c

    def start_queries(k, c):
        for h in (own0 + k, oth0 + k):
            load(q_hbm, q_buf, q_sem, h).start()
        return c

    rates_copy = pltpu.make_async_copy(rates_hbm, rates, r_sem)
    rates_copy.start()
    lax.fori_loop(0, half, start_states, 0)
    lax.fori_loop(0, half, start_queries, 0)

    barrier = pltpu.get_barrier_semaphore()

    def greet(seq, head):
        pl.semaphore_signal(
            barrier, inc=1, device_id={"seq": seq, "head": head}, device_id_type=pl.DeviceIdType.MESH
        )

    greet(core_peer, way)
    greet(x_peer, way)
    for d in range(1, ways):
        greet(me, lax.rem(way + d, ways))

    @pl.when(z > 0)
    def _():
        greet(me - GROUP, way)

    @pl.when(z < groups - 1)
    def _():
        greet(me + GROUP, way)

    @pl.when(z == 0)
    def _():
        p_in[...] = jnp.zeros_like(p_in)

    acc[...] = jnp.zeros_like(acc)
    rates_copy.wait()

    def power(rate, steps):
        return jnp.exp(jnp.full((1, E), -rate * steps, F32))

    row = lax.broadcasted_iota(jnp.int32, (8, E), 0).astype(F32)

    def rising(rate):
        column = jnp.exp(-rate * (row + 1.0))
        while column.shape[0] < BLOCK:
            column = jnp.concatenate([column, column * power(rate, float(column.shape[0]))], axis=0)
        return column

    def falling(rate):
        column = jnp.exp(-rate * (7.0 - row))
        while column.shape[0] < BLOCK:
            column = jnp.concatenate([column * power(rate, float(column.shape[0])), column], axis=0)
        return column


    def local_states(k):
        pair = (oth0 + k, own0 + k)
        for h in pair:
            load(k_hbm, k_buf, k_sem, h).wait()
            load(v_hbm, v_buf, v_sem, h).wait()
        whole = [power(rates[h], float(BLOCK)) for h in pair]
        scale = [falling(rates[h]) for h in pair]
        state = [None, None]
        for b in range(blocks):
            rows = pl.ds(b * BLOCK, BLOCK)
            for n, h in enumerate(pair):
                scaled = (k_buf[h, rows, :].astype(F32) * scale[n]).astype(BF16)
                part = dot(scaled, v_buf[h, rows, :], (0, 0))
                state[n] = part if b == 0 else state[n] * whole[n] + part
                if b < blocks - 1:
                    entering[h, b] = state[n]
                else:
                    s_loc[h] = state[n]

    def chip_total(k):
        rate = rates[own0 + k]
        state_copy(k).wait_recv()
        mine = power(rate, length * (1.0 - core_f))
        other = power(rate, length * core_f)
        c_tot[k] = mine * s_loc[own0 + k] + other * s_oth[k]

        @pl.when(lax.rem(k, 2) != x)
        def _():
            chip_copy(k // 2).start()

    def state_step(k, c):
        local_states(k)
        state_copy(k).start()
        chip_total(k - 1)
        return c

    local_states(0)
    pl.semaphore_wait(barrier, 2 + (ways - 1) + jnp.minimum(z, 1) + jnp.minimum(groups - 1 - z, 1))
    state_copy(0).start()
    lax.fori_loop(1, half, state_step, 0)
    chip_total(half - 1)

    small = E
    down = lax.broadcasted_iota(jnp.int32, (small, small), 0) - lax.broadcasted_iota(jnp.int32, (small, small), 1)
    down_f = down.astype(F32)
    left = (small - 1) - lax.broadcasted_iota(jnp.int32, (1, small), 1).astype(F32)
    blank = jnp.zeros((small, small), BF16)

    def attend(k):
        pair = (own0 + k, oth0 + k)
        for h in pair:
            load(q_hbm, q_buf, q_sem, h).wait()
        near = [jnp.where(down >= 0, jnp.exp(-rates[h] * jnp.maximum(down_f, 0.0)), 0.0) for h in pair]
        far = [rising(rates[h])[:small] * jnp.exp(-rates[h] * left) for h in pair]
        units = [(n, b) for n in range(2) for b in range(blocks)]

        def score(unit):
            rows = pl.ds(unit[1] * BLOCK, BLOCK)
            return dot(q_buf[pair[unit[0]], rows, :], k_buf[pair[unit[0]], rows, :], (1, 1))

        ahead = score(units[0])
        for at, (n, b) in enumerate(units):
            scores = ahead
            if at + 1 < len(units):
                ahead = score(units[at + 1])
            vals = v_buf[pair[n], pl.ds(b * BLOCK, BLOCK), :]
            top = jnp.concatenate([(scores[:small, :small] * near[n]).astype(BF16), blank], axis=1)
            low = jnp.concatenate(
                [(scores[small:, :small] * far[n]).astype(BF16), (scores[small:, small:] * near[n]).astype(BF16)],
                axis=1,
            )
            local[pair[n], pl.ds(b * BLOCK, BLOCK), :] = dot(jnp.concatenate([top, low], axis=0), vals, (1, 0))

    def share(k, chip):
        length_on = power(rates[own0 + k], float(length))

        @pl.when(core == 0)
        def _():
            e_mine[k] = chip
            e_send[k] = length_on * chip + s_loc[own0 + k]

        @pl.when(core == 1)
        def _():
            e_mine[k] = length_on * chip + s_oth[k]
            e_send[k] = chip

        carry_copy(k).start()

    def chain(m):
        k = 2 * m + x
        rate = rates[own0 + k]
        chip_copy(m).wait_recv()

        @pl.when(z > 0)
        def _():
            chain_copy(m).wait_recv()

        before = p_in[m]
        mine = c_tot[k]
        other = c_oth[m]
        chip_on = power(rate, 2.0 * length)
        second = chip_on * before + ((1.0 - x_f) * mine + x_f * other)

        @pl.when(z < groups - 1)
        def _():
            p_out[m] = chip_on * second + (x_f * mine + (1.0 - x_f) * other)
            chain_copy(m).start()

        g_out[m] = x_f * before + (1.0 - x_f) * second
        return_copy(m).start()
        share(k, (1.0 - x_f) * before + x_f * second)

    def relay(m):
        return_copy(m).wait_recv()
        share(2 * m + 1 - x, g_in[m])

    def finish(k):
        pair = (own0 + k, oth0 + k)
        carry_copy(k).wait_recv()
        carry = (e_mine[k], e_oth[k])
        scale = [rising(rates[h]) for h in pair]
        units = [(n, b) for b in range(blocks) for n in range(2)]

        def carried(unit):
            n, b = unit
            h = pair[n]
            state = carry[n]
            if b > 0:
                state = power(rates[h], float(b * BLOCK)) * state + entering[h, b - 1]
            return dot(q_buf[h, pl.ds(b * BLOCK, BLOCK), :], state.astype(BF16), (1, 0))

        ahead = carried(units[0])
        squares = None
        for at, (n, b) in enumerate(units):
            now = ahead
            if at + 1 < len(units):
                ahead = carried(units[at + 1])
            rows = pl.ds(b * BLOCK, BLOCK)
            mixed = local[pair[n], rows, :] + scale[n] * now
            mix[pair[n], rows, :] = mixed
            squares = mixed * mixed if n == 0 else squares + mixed * mixed
            if n == 1:
                acc[rows, :] += squares

    lag = jnp.minimum(2 * z, half - (quarter + 1) // 2)

    def step(i, c):
        attend(i)

        def turn(n, c):
            m = 2 * (i - lag) + n

            @pl.when(jnp.logical_and(m >= 0, m < quarter))
            def _():
                chain(m)

            return c

        return lax.fori_loop(0, 2, turn, c)

    def owned(t, c):
        @pl.when(t < quarter)
        def _():
            finish(2 * t + x)

        @pl.when(t > 0)
        def _():
            relay(t - 1)

        return c

    def relayed(t, c):
        finish(2 * t + 1 - x)
        return c

    lax.fori_loop(0, half, step, 0)
    lax.fori_loop(0, quarter + 1, owned, 0)
    lax.fori_loop(0, quarter, relayed, 0)

    slabs = length // E
    for g in range(slabs):
        ss_loc[pl.ds(g, 1), :] = jnp.sum(acc[pl.ds(g * E, E), :].T, axis=0, keepdims=True)
    for d in range(1, ways):
        norm_copy(d).start()
    for d in range(1, ways):
        norm_copy(d).wait_recv()
    sums = ss_loc[...]
    for d in range(1, ways):
        sums = sums + ss_in[d - 1]
    sums_ref[...] = sums

    def drain(k, c):
        state_copy(k).wait_send()
        carry_copy(k).wait_send()
        return c

    def drain_links(m, c):
        chip_copy(m).wait_send()
        return_copy(m).wait_send()

        @pl.when(z < groups - 1)
        def _():
            chain_copy(m).wait_send()

        return c

    lax.fori_loop(0, quarter, drain_links, 0)
    lax.fori_loop(0, half, drain, 0)
    for d in range(1, ways):
        norm_copy(d).wait_send()


def normalise(width, mixed_ref, sums_ref, gain_hbm, out_hbm, gain, ready, gain_sem, out_sem):
    slabs = mixed_ref.shape[1] // E
    fetch = pltpu.make_async_copy(gain_hbm, gain, gain_sem)
    fetch.start()

    def put(t):
        rows = pl.ds(pl.multiple_of(t * E, E), E)
        return pltpu.make_async_copy(ready.at[rows], out_hbm.at[rows], out_sem.at[t])

    fetch.wait()

    def slab(t, c):
        inverse = jnp.broadcast_to(lax.rsqrt(sums_ref[pl.ds(t, 1), :] / width + EPSILON), (E, E)).T
        rows = pl.ds(pl.multiple_of(t * E, E), E)
        for h in range(mixed_ref.shape[0]):
            cols = pl.ds(h * E, E)
            ready[rows, cols] = (mixed_ref[h, rows, :] * inverse * gain[:, cols]).astype(BF16)
        put(t).start()
        return c

    lax.fori_loop(0, slabs, slab, 0)

    def drain(t, c):
        put(t).wait()
        return c

    lax.fori_loop(0, slabs, drain, 0)


def body(runs, ways, queries, key_rows, value_rows, decay_rates, out_gain):
    length, columns = queries.shape
    heads = decay_rates.shape[0]
    half = heads // 2
    quarter = half // 2
    blocks = length // BLOCK
    dma = pltpu.SemaphoreType.DMA
    states = [pltpu.VMEM((half, E, E), F32)]
    sems = [dma((half,))]
    fixed = [pltpu.with_memory_space_constraint(a, pltpu.HBM) for a in (queries, key_rows, value_rows, decay_rates)]
    gain = pltpu.with_memory_space_constraint(out_gain.reshape(1, columns), pltpu.HBM)
    sums_shape = (length // E, E)
    mixed, sums = pl.pallas_call(
        functools.partial(kernel, runs, ways),
        out_shape=(jax.ShapeDtypeStruct((heads, length, E), F32), jax.ShapeDtypeStruct(sums_shape, F32)),
        in_specs=[pl.BlockSpec(memory_space=pltpu.HBM)] * 4,
        out_specs=(pl.BlockSpec(memory_space=pltpu.VMEM),) * 2,
        scratch_shapes=[pltpu.SMEM((heads,), F32)]
        + [pltpu.VMEM((heads, length, E), BF16)] * 3
        + [
            pltpu.VMEM((heads, length, E), F32),
            pltpu.VMEM((length, E), F32),
            pltpu.VMEM((heads, blocks - 1, E, E), F32),
            pltpu.VMEM((heads, E, E), F32),
        ]
        + states
        + states
        + [pltpu.VMEM((quarter, E, E), F32)] * 5
        + states * 3
        + [pltpu.VMEM(sums_shape, F32), pltpu.VMEM((max(ways - 1, 1),) + sums_shape, F32)]
        + [dma]
        + [dma((heads,))] * 3
        + sems * 2
        + [dma((quarter,))] * 6
        + sems * 2
        + [dma((max(ways - 1, 1),))] * 2,
        compiler_params=pltpu.CompilerParams(
            collective_id=0, has_side_effects=True, vmem_limit_bytes=40 * 1024 * 1024
        ),
        cost_estimate=pl.CostEstimate(
            flops=12 * length * BLOCK * heads * E, bytes_accessed=8 * length * heads * E, transcendentals=0
        ),
    )(*fixed)
    return pl.pallas_call(
        functools.partial(normalise, float(heads * ways * E)),
        out_shape=jax.ShapeDtypeStruct(queries.shape, BF16),
        in_specs=[pl.BlockSpec(memory_space=pltpu.VMEM)] * 2 + [pl.BlockSpec(memory_space=pltpu.HBM)],
        out_specs=pl.BlockSpec(memory_space=pltpu.HBM),
        scratch_shapes=[
            pltpu.VMEM((1, columns), F32),
            pltpu.VMEM(queries.shape, BF16),
            dma,
            dma((length // E,)),
        ],
        compiler_params=pltpu.CompilerParams(vmem_limit_bytes=16 * 1024 * 1024),
        cost_estimate=pl.CostEstimate(
            flops=3 * length * columns, bytes_accessed=4 * length * columns, transcendentals=0
        ),
    )(mixed, sums, gain)


def solution(mesh):
    placed = (P("seq", "head"), P("seq", "head"), P("seq", "head"), P("head"), P("head"))
    return jax.shard_map(
        functools.partial(body, mesh.shape["seq"], mesh.shape["head"]),
        mesh=mesh, in_specs=placed, out_specs=P("seq", "head"), check_vma=False,
    )
```

```python
import functools

import jax
import jax.numpy as jnp
from jax import lax
from jax.experimental import pallas as pl
from jax.experimental.pallas import tpu as pltpu
from jax.sharding import PartitionSpec as P

E = 128
BLOCK = 256
EPSILON = 1e-06
GROUP = 4
F32 = jnp.float32
BF16 = jnp.bfloat16


def dot(a, b, contract):
    return lax.dot_general(a, b, ((contract[:1], contract[1:]), ((), ())), preferred_element_type=F32)


def kernel(
    runs, ways,
    q_hbm, k_hbm, v_hbm, rates_hbm, mix, sums_ref,
    rates, q_buf, k_buf, v_buf, local, acc, entering,
    s_loc, s_oth, c_tot, c_oth, p_in, p_out, g_out, g_in, e_mine, e_send, e_oth, ss_loc, ss_in,
    r_sem, q_sem, k_sem, v_sem, s_ss, s_rs, c_ss, c_rs, p_ss, p_rs, g_ss, g_rs, e_ss, e_rs, n_ss, n_rs,
):
    heads, length = q_buf.shape[0], q_buf.shape[1]
    half = heads // 2
    quarter = half // 2
    blocks = length // BLOCK
    groups = runs // GROUP
    me = lax.axis_index("seq")
    way = lax.axis_index("head")
    core = lax.rem(me, 2)
    x = lax.rem(me // 2, 2)
    z = me // GROUP
    core_peer = me + 1 - 2 * core
    x_peer = me + 2 - 4 * x
    own0 = core * half
    oth0 = (1 - core) * half
    core_f = core.astype(F32)
    x_f = x.astype(F32)

    def load(hbm, buf, sem, h):
        return pltpu.make_async_copy(hbm.at[:, pl.ds(pl.multiple_of(h * E, E), E)], buf.at[h], sem.at[h])

    def remote(src, dst, ss, rs, seq, head):
        return pltpu.make_async_remote_copy(
            src_ref=src, dst_ref=dst, send_sem=ss, recv_sem=rs,
            device_id={"seq": seq, "head": head}, device_id_type=pl.DeviceIdType.MESH,
        )

    def state_copy(k):
        return remote(s_loc.at[oth0 + k], s_oth.at[k], s_ss.at[k], s_rs.at[k], core_peer, way)

    def chip_copy(m):
        return remote(c_tot.at[2 * m + 1 - x], c_oth.at[m], c_ss.at[m], c_rs.at[m], x_peer, way)

    def chain_copy(m):
        up = lax.rem(me + GROUP, runs)
        return remote(p_out.at[m], p_in.at[m], p_ss.at[m], p_rs.at[m], up, way)

    def return_copy(m):
        return remote(g_out.at[m], g_in.at[m], g_ss.at[m], g_rs.at[m], x_peer, way)

    def carry_copy(k):
        return remote(e_send.at[k], e_oth.at[k], e_ss.at[k], e_rs.at[k], core_peer, way)

    def norm_copy(d):
        return remote(ss_loc, ss_in.at[d - 1], n_ss.at[d - 1], n_rs.at[d - 1], me, lax.rem(way + d, ways))

    def start_states(k, c):
        for h in (own0 + k, oth0 + k):
            load(k_hbm, k_buf, k_sem, h).start()
            load(v_hbm, v_buf, v_sem, h).start()
        return c

    def start_queries(k, c):
        for h in (own0 + k, oth0 + k):
            load(q_hbm, q_buf, q_sem, h).start()
        return c

    rates_copy = pltpu.make_async_copy(rates_hbm, rates, r_sem)
    rates_copy.start()
    lax.fori_loop(0, half, start_states, 0)
    lax.fori_loop(0, half, start_queries, 0)

    barrier = pltpu.get_barrier_semaphore()

    def greet(seq, head):
        pl.semaphore_signal(
            barrier, inc=1, device_id={"seq": seq, "head": head}, device_id_type=pl.DeviceIdType.MESH
        )

    greet(core_peer, way)
    greet(x_peer, way)
    for d in range(1, ways):
        greet(me, lax.rem(way + d, ways))

    @pl.when(z > 0)
    def _():
        greet(me - GROUP, way)

    @pl.when(z < groups - 1)
    def _():
        greet(me + GROUP, way)

    @pl.when(z == 0)
    def _():
        p_in[...] = jnp.zeros_like(p_in)

    acc[...] = jnp.zeros_like(acc)
    rates_copy.wait()

    def power(rate, steps):
        return jnp.exp(jnp.full((1, E), -rate * steps, F32))

    row = lax.broadcasted_iota(jnp.int32, (8, E), 0).astype(F32)

    def rising(rate):
        column = jnp.exp(-rate * (row + 1.0))
        while column.shape[0] < BLOCK:
            column = jnp.concatenate([column, column * power(rate, float(column.shape[0]))], axis=0)
        return column

    def falling(rate):
        column = jnp.exp(-rate * (7.0 - row))
        while column.shape[0] < BLOCK:
            column = jnp.concatenate([column * power(rate, float(column.shape[0])), column], axis=0)
        return column


    def local_states(k):
        pair = (oth0 + k, own0 + k)
        for h in pair:
            load(k_hbm, k_buf, k_sem, h).wait()
            load(v_hbm, v_buf, v_sem, h).wait()
        whole = [power(rates[h], float(BLOCK)) for h in pair]
        scale = [falling(rates[h]) for h in pair]
        state = [None, None]
        for b in range(blocks):
            rows = pl.ds(b * BLOCK, BLOCK)
            for n, h in enumerate(pair):
                scaled = (k_buf[h, rows, :].astype(F32) * scale[n]).astype(BF16)
                part = dot(scaled, v_buf[h, rows, :], (0, 0))
                state[n] = part if b == 0 else state[n] * whole[n] + part
                if b < blocks - 1:
                    entering[h, b] = state[n]
                else:
                    s_loc[h] = state[n]

    def chip_total(k):
        rate = rates[own0 + k]
        state_copy(k).wait_recv()
        mine = power(rate, length * (1.0 - core_f))
        other = power(rate, length * core_f)
        c_tot[k] = mine * s_loc[own0 + k] + other * s_oth[k]

        @pl.when(lax.rem(k, 2) != x)
        def _():
            chip_copy(k // 2).start()

    def state_step(k, c):
        local_states(k)
        state_copy(k).start()
        chip_total(k - 1)
        return c

    local_states(0)
    pl.semaphore_wait(barrier, 2 + (ways - 1) + jnp.minimum(z, 1) + jnp.minimum(groups - 1 - z, 1))
    state_copy(0).start()
    lax.fori_loop(1, half, state_step, 0)
    chip_total(half - 1)

    small = E
    down = lax.broadcasted_iota(jnp.int32, (small, small), 0) - lax.broadcasted_iota(jnp.int32, (small, small), 1)
    down_f = down.astype(F32)
    left = (small - 1) - lax.broadcasted_iota(jnp.int32, (1, small), 1).astype(F32)
    blank = jnp.zeros((small, small), BF16)

    def attend(k):
        pair = (own0 + k, oth0 + k)
        for h in pair:
            load(q_hbm, q_buf, q_sem, h).wait()
        near = [jnp.where(down >= 0, jnp.exp(-rates[h] * jnp.maximum(down_f, 0.0)), 0.0) for h in pair]
        far = [rising(rates[h])[:small] * jnp.exp(-rates[h] * left) for h in pair]
        units = [(n, b) for n in range(2) for b in range(blocks)]

        def score(unit):
            rows = pl.ds(unit[1] * BLOCK, BLOCK)
            return dot(q_buf[pair[unit[0]], rows, :], k_buf[pair[unit[0]], rows, :], (1, 1))

        ahead = score(units[0])
        for at, (n, b) in enumerate(units):
            scores = ahead
            if at + 1 < len(units):
                ahead = score(units[at + 1])
            vals = v_buf[pair[n], pl.ds(b * BLOCK, BLOCK), :]
            top = jnp.concatenate([(scores[:small, :small] * near[n]).astype(BF16), blank], axis=1)
            low = jnp.concatenate(
                [(scores[small:, :small] * far[n]).astype(BF16), (scores[small:, small:] * near[n]).astype(BF16)],
                axis=1,
            )
            local[pair[n], pl.ds(b * BLOCK, BLOCK), :] = dot(jnp.concatenate([top, low], axis=0), vals, (1, 0))

    def share(k, chip):
        length_on = power(rates[own0 + k], float(length))

        @pl.when(core == 0)
        def _():
            e_mine[k] = chip
            e_send[k] = length_on * chip + s_loc[own0 + k]

        @pl.when(core == 1)
        def _():
            e_mine[k] = length_on * chip + s_oth[k]
            e_send[k] = chip

        carry_copy(k).start()

    def chain(m):
        k = 2 * m + x
        rate = rates[own0 + k]
        chip_copy(m).wait_recv()

        @pl.when(z > 0)
        def _():
            chain_copy(m).wait_recv()

        before = p_in[m]
        mine = c_tot[k]
        other = c_oth[m]
        chip_on = power(rate, 2.0 * length)
        second = chip_on * before + ((1.0 - x_f) * mine + x_f * other)

        @pl.when(z < groups - 1)
        def _():
            p_out[m] = chip_on * second + (x_f * mine + (1.0 - x_f) * other)
            chain_copy(m).start()

        g_out[m] = x_f * before + (1.0 - x_f) * second
        return_copy(m).start()
        share(k, (1.0 - x_f) * before + x_f * second)

    def relay(m):
        return_copy(m).wait_recv()
        share(2 * m + 1 - x, g_in[m])

    def finish(k):
        pair = (own0 + k, oth0 + k)
        carry_copy(k).wait_recv()
        carry = (e_mine[k], e_oth[k])
        scale = [rising(rates[h]) for h in pair]
        units = [(n, b) for b in range(blocks) for n in range(2)]

        def carried(unit):
            n, b = unit
            h = pair[n]
            state = carry[n]
            if b > 0:
                state = power(rates[h], float(b * BLOCK)) * state + entering[h, b - 1]
            return dot(q_buf[h, pl.ds(b * BLOCK, BLOCK), :], state.astype(BF16), (1, 0))

        ahead = carried(units[0])
        squares = None
        for at, (n, b) in enumerate(units):
            now = ahead
            if at + 1 < len(units):
                ahead = carried(units[at + 1])
            rows = pl.ds(b * BLOCK, BLOCK)
            mixed = local[pair[n], rows, :] + scale[n] * now
            mix[pair[n], rows, :] = mixed
            squares = mixed * mixed if n == 0 else squares + mixed * mixed
            if n == 1:
                acc[rows, :] += squares

    lag = jnp.minimum(3 * z, half)

    def step(i, c):
        def turn(n, c):
            m = 2 * (i - lag) + n

            @pl.when(jnp.logical_and(m >= 0, m < quarter))
            def _():
                chain(m)

            return c

        lax.fori_loop(0, 2, turn, 0)

        @pl.when(i < half)
        def _():
            attend(i)

        t = i - half

        @pl.when(jnp.logical_and(t >= 0, t < quarter))
        def _():
            finish(2 * t + x)

        @pl.when(t > 0)
        def _():
            relay(t - 1)

        return c

    def relayed(t, c):
        finish(2 * t + 1 - x)
        return c

    lax.fori_loop(0, half + quarter + 1, step, 0)
    lax.fori_loop(0, quarter, relayed, 0)

    slabs = length // E
    for g in range(slabs):
        ss_loc[pl.ds(g, 1), :] = jnp.sum(acc[pl.ds(g * E, E), :].T, axis=0, keepdims=True)
    for d in range(1, ways):
        norm_copy(d).start()
    for d in range(1, ways):
        norm_copy(d).wait_recv()
    sums = ss_loc[...]
    for d in range(1, ways):
        sums = sums + ss_in[d - 1]
    sums_ref[...] = sums

    def drain(k, c):
        state_copy(k).wait_send()
        carry_copy(k).wait_send()
        return c

    def drain_links(m, c):
        chip_copy(m).wait_send()
        return_copy(m).wait_send()

        @pl.when(z < groups - 1)
        def _():
            chain_copy(m).wait_send()

        return c

    lax.fori_loop(0, quarter, drain_links, 0)
    lax.fori_loop(0, half, drain, 0)
    for d in range(1, ways):
        norm_copy(d).wait_send()


def normalise(width, mixed_ref, sums_ref, gain_hbm, out_hbm, gain, ready, gain_sem, out_sem):
    slabs = mixed_ref.shape[1] // E
    fetch = pltpu.make_async_copy(gain_hbm, gain, gain_sem)
    fetch.start()

    def put(t):
        rows = pl.ds(pl.multiple_of(t * E, E), E)
        return pltpu.make_async_copy(ready.at[rows], out_hbm.at[rows], out_sem.at[t])

    fetch.wait()

    def slab(t, c):
        inverse = jnp.broadcast_to(lax.rsqrt(sums_ref[pl.ds(t, 1), :] / width + EPSILON), (E, E)).T
        rows = pl.ds(pl.multiple_of(t * E, E), E)
        for h in range(mixed_ref.shape[0]):
            cols = pl.ds(h * E, E)
            ready[rows, cols] = (mixed_ref[h, rows, :] * inverse * gain[:, cols]).astype(BF16)
        put(t).start()
        return c

    lax.fori_loop(0, slabs, slab, 0)

    def drain(t, c):
        put(t).wait()
        return c

    lax.fori_loop(0, slabs, drain, 0)


def body(runs, ways, queries, key_rows, value_rows, decay_rates, out_gain):
    length, columns = queries.shape
    heads = decay_rates.shape[0]
    half = heads // 2
    quarter = half // 2
    blocks = length // BLOCK
    dma = pltpu.SemaphoreType.DMA
    states = [pltpu.VMEM((half, E, E), F32)]
    sems = [dma((half,))]
    fixed = [pltpu.with_memory_space_constraint(a, pltpu.HBM) for a in (queries, key_rows, value_rows, decay_rates)]
    gain = pltpu.with_memory_space_constraint(out_gain.reshape(1, columns), pltpu.HBM)
    sums_shape = (length // E, E)
    mixed, sums = pl.pallas_call(
        functools.partial(kernel, runs, ways),
        out_shape=(jax.ShapeDtypeStruct((heads, length, E), F32), jax.ShapeDtypeStruct(sums_shape, F32)),
        in_specs=[pl.BlockSpec(memory_space=pltpu.HBM)] * 4,
        out_specs=(pl.BlockSpec(memory_space=pltpu.VMEM),) * 2,
        scratch_shapes=[pltpu.SMEM((heads,), F32)]
        + [pltpu.VMEM((heads, length, E), BF16)] * 3
        + [
            pltpu.VMEM((heads, length, E), F32),
            pltpu.VMEM((length, E), F32),
            pltpu.VMEM((heads, blocks - 1, E, E), F32),
            pltpu.VMEM((heads, E, E), F32),
        ]
        + states
        + states
        + [pltpu.VMEM((quarter, E, E), F32)] * 5
        + states * 3
        + [pltpu.VMEM(sums_shape, F32), pltpu.VMEM((max(ways - 1, 1),) + sums_shape, F32)]
        + [dma]
        + [dma((heads,))] * 3
        + sems * 2
        + [dma((quarter,))] * 6
        + sems * 2
        + [dma((max(ways - 1, 1),))] * 2,
        compiler_params=pltpu.CompilerParams(
            collective_id=0, has_side_effects=True, vmem_limit_bytes=40 * 1024 * 1024
        ),
        cost_estimate=pl.CostEstimate(
            flops=12 * length * BLOCK * heads * E, bytes_accessed=8 * length * heads * E, transcendentals=0
        ),
    )(*fixed)
    return pl.pallas_call(
        functools.partial(normalise, float(heads * ways * E)),
        out_shape=jax.ShapeDtypeStruct(queries.shape, BF16),
        in_specs=[pl.BlockSpec(memory_space=pltpu.VMEM)] * 2 + [pl.BlockSpec(memory_space=pltpu.HBM)],
        out_specs=pl.BlockSpec(memory_space=pltpu.HBM),
        scratch_shapes=[
            pltpu.VMEM((1, columns), F32),
            pltpu.VMEM(queries.shape, BF16),
            dma,
            dma((length // E,)),
        ],
        compiler_params=pltpu.CompilerParams(vmem_limit_bytes=16 * 1024 * 1024),
        cost_estimate=pl.CostEstimate(
            flops=3 * length * columns, bytes_accessed=4 * length * columns, transcendentals=0
        ),
    )(mixed, sums, gain)


def solution(mesh):
    placed = (P("seq", "head"), P("seq", "head"), P("seq", "head"), P("head"), P("head"))
    return jax.shard_map(
        functools.partial(body, mesh.shape["seq"], mesh.shape["head"]),
        mesh=mesh, in_specs=placed, out_specs=P("seq", "head"), check_vma=False,
    )
```
